256 devices in a mesh: segment: 4 (over y), dp: 64 (over x, z, core).
Axes of the slice: x: 4, y: 4, z: 8, core: 2. Of those that a mesh axis runs over, the one named last changes fastest.
Arguments:
- images: bfloat16 [2, 512, 32, 768], P(None, 'dp'), may hold values from -6 to 6
- dw_weight: bfloat16 [4, 7, 7, 768], P('segment'), may hold values from -0.875 to 0.875
- dw_bias: float32 [4, 768], P('segment'), may hold values from -3 to 3
- ln_gain: float32 [4, 768], P('segment'), may hold values from 0.5 to 2
- ln_bias: float32 [4, 768], P('segment'), may hold values from -3 to 3
- w_in: bfloat16 [4, 768, 3072], P('segment'), may hold values from -0.21875 to 0.21875
- b_in: float32 [4, 3072], P('segment'), may hold values from -3 to 3
- w_out: bfloat16 [4, 3072, 768], P('segment'), may hold values from -0.109375 to 0.109375
- b_out: float32 [4, 768], P('segment'), may hold values from -3 to 3
- layer_scale: float32 [4, 768], P('segment'), may hold values from 0.25 to 1
Outputs:
- stash: bfloat16 [4, 2, 512, 32, 768], P('segment', None, 'dp')
The draws below stay inside these ranges and needn't reach their ends.
All inputs are finite; a program needn't handle non-finite values.
Results may differ from the reference program's by a relative error of at most 0.015.
Values may be sent and summed in bfloat16 or wider, within the bound.
No kernel may reach another device: no remote copies, remote signals or barrier semaphores. Data moves between devices by JAX's collectives and lax.ppermute only.
A program may use at most 128 MiB of HBM per device.

```python
import math
import jax
import jax.numpy as jnp
from jax import lax

C = 768
HID = 3072
SIDE = 32
MICRO = 2
BLOCKS = 4
ROWS = 512


def level_of(key, shape, cuts, least, largest):
    def one(dim, blocks):
        steps = jax.random.uniform(jax.random.fold_in(jax.random.fold_in(key, 6), dim), (blocks,), jnp.float32, least / len(cuts), largest / len(cuts))
        return jnp.repeat(jnp.exp(steps), shape[dim] // blocks).reshape((-1,) + (1,) * (len(shape) - dim - 1))

    level = one(*cuts[0])
    for cut in cuts[1:]:
        level = level * one(*cut)
    return level


def bell_draw(own_key, extent, scale, bound, cuts=(), kind=jnp.bfloat16):
    loudness = level_of(own_key, extent, cuts, -0.22, 0.18) if cuts else 1.0
    values = jax.random.normal(own_key, extent, jnp.float32) * scale * loudness
    return jnp.minimum(jnp.maximum(values, -bound), bound).astype(kind)


def setup_inputs(seed: int = 0) -> dict:
    arg_keys = jax.random.split(jax.random.key(seed), 11)
    return {
        "images": bell_draw(arg_keys[0], (MICRO, ROWS, SIDE, C), 1.0, 6.0, ((1, 64),)),
        "dw_weight": bell_draw(arg_keys[1], (BLOCKS, 7, 7, C), 49 ** -0.5, 0.875, ((0, 4),)),
        "dw_bias": bell_draw(arg_keys[2], (BLOCKS, C), 0.5, 3.0, ((0, 4),), jnp.float32),
        "ln_gain": jnp.clip(jnp.exp(math.log(2.0) - 1.3862944 * jax.random.uniform(arg_keys[3], (BLOCKS, C), jnp.float32) ** level_of(arg_keys[3], (BLOCKS, C), ((0, 4),), -0.2, 0.2)), 0.5, 2.0),
        "ln_bias": bell_draw(arg_keys[4], (BLOCKS, C), 0.5, 3.0, ((0, 4),), jnp.float32),
        "w_in": bell_draw(arg_keys[5], (BLOCKS, C, HID), C ** -0.5, 0.21875, ((0, 4),)),
        "b_in": bell_draw(arg_keys[6], (BLOCKS, HID), 0.5, 3.0, ((0, 4),), jnp.float32),
        "w_out": bell_draw(arg_keys[7], (BLOCKS, HID, C), HID ** -0.5, 0.109375, ((0, 4),)),
        "b_out": bell_draw(arg_keys[8], (BLOCKS, C), 0.5, 3.0, ((0, 4),), jnp.float32),
        "layer_scale": jnp.clip(jnp.exp(math.log(1.0) - 1.3862944 * jax.random.uniform(arg_keys[9], (BLOCKS, C), jnp.float32) ** level_of(arg_keys[9], (BLOCKS, C), ((0, 4),), -0.2, 0.2)), 0.25, 1.0),
    }


def depthwise(field, weight, bias):
    half = SIDE // 2
    rolled = jnp.roll(field.astype(jnp.float32), half, axis=0)
    maps = rolled.reshape(-1, SIDE, SIDE, field.shape[-1])
    padded = jnp.pad(maps, ((0, 0), (3, 3), (3, 3), (0, 0)))
    total = jnp.zeros(maps.shape, jnp.float32)
    for row_off in range(7):
        for col_off in range(7):
            total = total + padded[:, row_off:row_off + SIDE, col_off:col_off + SIDE, :] * weight[row_off, col_off].astype(jnp.float32)
    total = total + bias
    total = jnp.roll(total.reshape(field.shape), -half, axis=0)
    return total.astype(jnp.bfloat16)

def convnext_block(field, dww, dwb, gain, shift, win, bin_, wout, bout, scale):
    conv = depthwise(field, dww, dwb).astype(jnp.float32)
    mean = lax.optimization_barrier(jnp.mean(conv, axis=-1, keepdims=True))
    var = lax.optimization_barrier(jnp.mean((conv - mean) ** 2, axis=-1, keepdims=True))
    normalized = ((conv - mean) * jax.lax.rsqrt(var + 1e-06) * gain + shift).astype(jnp.bfloat16)
    flat = normalized.reshape(-1, field.shape[-1])
    hidden = jax.nn.gelu(jnp.dot(flat, win, preferred_element_type=jnp.float32) + bin_, approximate=False).astype(jnp.bfloat16)
    branch = jnp.dot(hidden, wout, preferred_element_type=jnp.float32) + bout
    result = field.astype(jnp.float32) + scale * branch.reshape(field.shape)
    return result.astype(jnp.bfloat16)

def reference(images, dw_weight, dw_bias, ln_gain, ln_bias, w_in, b_in, w_out, b_out, layer_scale):
    outputs = []
    for block in range(BLOCKS):
        row = []
        for micro in range(MICRO):
            source = images[micro] if block == 0 else outputs[block - 1][micro]
            row.append(convnext_block(source, dw_weight[block], dw_bias[block], ln_gain[block], ln_bias[block], w_in[block], b_in[block], w_out[block], b_out[block], layer_scale[block]))
        outputs.append(row)
    return jnp.stack([jnp.stack(row) for row in outputs])
```

```python
import functools

import jax
import jax.numpy as jnp
import numpy as np
from jax import lax
from jax.experimental import pallas as pl
from jax.experimental.pallas import tpu as pltpu
from jax.sharding import PartitionSpec as P

SIDE = 32
TAPS = 7
REACH = 3
LANES = 128
NEAR = 3
BF = jnp.bfloat16
F32 = jnp.float32


def block_kernel(
    micro, chunk, flags, near, far, swap, cross, taps, conv_bias, gain, shift, select, b_in, b_out, scale, w_in_hbm,
    w_out_hbm, *rest,
):
    stash, near_out, far_out, cross_out, w_in, w_out, sums, normal, total, result, sems = rest[-11:]
    rows, width, channels = result.shape
    hidden = w_in.shape[1]

    def source(row, lanes):
        if row < REACH:
            return swap[REACH - 1 - row, :, lanes]
        if row < REACH + NEAR:
            return near[row - REACH, :, lanes]
        if row < REACH + rows:
            return far[row - REACH - NEAR, :, lanes]
        return cross[2 * REACH + rows - 1 - row, :, lanes]

    @pl.when(flags[0] == 1)
    def _():
        get_in = pltpu.make_async_copy(w_in_hbm, w_in, sems.at[0])
        get_out = pltpu.make_async_copy(w_out_hbm, w_out, sems.at[1])
        get_in.start()
        get_out.start()
        for group in range(channels // LANES):
            lanes = slice(group * LANES, (group + 1) * LANES)
            inputs = [source(row, lanes) for row in range(rows + 2 * REACH)]
            for col in range(TAPS):
                parts = [None] * rows
                for off in range(TAPS):
                    tap = taps[off * TAPS + col, :, lanes]
                    tap = jnp.concatenate([tap, tap], axis=0)
                    for row in range(rows):
                        term = inputs[row + off] * tap
                        parts[row] = term if off == 0 else parts[row] + term
                for row in range(rows):
                    sums[row, col * width : (col + 1) * width, lanes] = parts[row]
        for row in range(rows):
            conv = jnp.dot(select[...], sums[row], preferred_element_type=F32) + conv_bias[...]
            centred = conv - jnp.mean(conv, axis=-1, keepdims=True)
            var = jnp.mean(centred * centred, axis=-1, keepdims=True)
            normal[row * width : (row + 1) * width, :] = (
                centred * lax.rsqrt(var + 1e-06) * gain[...] + shift[...]
            ).astype(BF)
        get_in.wait()
        get_out.wait()
        for start in range(0, hidden, chunk):
            part = slice(start, start + chunk)
            inner = jnp.dot(normal[...], w_in[:, part], preferred_element_type=F32) + b_in[:, part]
            act = (0.5 * inner * (1.0 + lax.erf(inner * np.float32(0.5**0.5)))).astype(BF)
            branch = jnp.dot(act, w_out[part, :], preferred_element_type=F32)
            if start == 0:
                total[...] = branch
            else:
                total[...] += branch
        flip = flags[1]
        for row in range(rows):
            here = near[row] if row < NEAR else far[row - NEAR]
            value = here.astype(F32) + scale[...] * (total[row * width : (row + 1) * width, :] + b_out[...])
            value = value.astype(BF)
            if row < NEAR:
                near_out[row] = value
            else:
                far_out[row - NEAR] = value
            if row >= rows - REACH:
                cross_out[row - (rows - REACH)] = value
            result[flip * (rows - 1) + (1 - 2 * flip) * row] = value
        copy = pltpu.make_async_copy(result, stash.at[0, micro], sems.at[2])
        copy.start()
        copy.wait()


def rows_kernel(flags, images, near, far, cross, sems):
    rows = images.shape[0]
    flip = flags[1]
    copies = []
    for row in range(rows):
        here = images.at[flip * (rows - 1) + (1 - 2 * flip) * row]
        copies.append((here, near.at[row] if row < NEAR else far.at[row - NEAR]))
        if row >= rows - REACH:
            copies.append((here, cross.at[row - (rows - REACH)]))
    copies = [pltpu.make_async_copy(a, b, sems.at[i]) for i, (a, b) in enumerate(copies)]
    for copy in copies:
        copy.start()
    for copy in copies:
        copy.wait()


def mirrored_rows(flags, images):
    rows, width, channels = images.shape
    return pl.pallas_call(
        rows_kernel,
        out_shape=[
            pltpu.VMEM((NEAR, width, channels), BF),
            pltpu.VMEM((rows - NEAR, width, channels), BF),
            pltpu.VMEM((REACH, width, channels), BF),
        ],
        in_specs=[pl.BlockSpec(memory_space=pltpu.SMEM), pl.BlockSpec(memory_space=pl.ANY)],
        out_specs=[pl.BlockSpec(memory_space=pltpu.VMEM)] * 3,
        scratch_shapes=[pltpu.SemaphoreType.DMA((rows + REACH,))],
        compiler_params=pltpu.CompilerParams(vmem_limit_bytes=2**20),
        cost_estimate=pl.CostEstimate(flops=0, bytes_accessed=2 * rows * width * channels, transcendentals=0),
        name="mirrored_rows",
    )(flags, images)


def run_block(micro, micros, flags, halo, params, weights, stash):
    near, far, swap, cross = halo
    rows, width, channels = near.shape[0] + far.shape[0], near.shape[1], near.shape[2]
    hidden = weights[0].shape[1]
    vmem = pl.BlockSpec(memory_space=pltpu.VMEM)
    anywhere = pl.BlockSpec(memory_space=pl.ANY)
    operands = [pltpu.with_memory_space_constraint(v, pltpu.VMEM) for v in (near, far, swap, cross) + params]
    held = [pltpu.with_memory_space_constraint(v, pltpu.HBM) for v in weights]
    specs = [pl.BlockSpec(memory_space=pltpu.SMEM)] + [vmem] * len(operands)
    specs += [pl.BlockSpec(memory_space=pltpu.HBM)] * len(held)
    operands = [flags] + operands + held
    aliases = {}
    if stash is not None:
        aliases = {len(operands): 0}
        operands.append(stash)
        specs.append(anywhere)
    out = pl.pallas_call(
        functools.partial(block_kernel, micro, 768),
        out_shape=[
            jax.ShapeDtypeStruct((1, micros, rows, width, channels), BF),
            pltpu.VMEM((NEAR, width, channels), BF),
            pltpu.VMEM((rows - NEAR, width, channels), BF),
            pltpu.VMEM((REACH, width, channels), BF),
        ],
        in_specs=specs,
        out_specs=[anywhere, vmem, vmem, vmem],
        scratch_shapes=[
            pltpu.VMEM(weights[0].shape, BF),
            pltpu.VMEM(weights[1].shape, BF),
            pltpu.VMEM((rows, TAPS * width, channels), BF),
            pltpu.VMEM((rows * width, channels), BF),
            pltpu.VMEM((rows * width, channels), F32),
            pltpu.VMEM((rows, width, channels), BF),
            pltpu.SemaphoreType.DMA((3,)),
        ],
        input_output_aliases=aliases,
        compiler_params=pltpu.CompilerParams(vmem_limit_bytes=32 * 2**20),
        cost_estimate=pl.CostEstimate(
            flops=4 * rows * width * channels * hidden, bytes_accessed=4 * channels * hidden, transcendentals=0
        ),
        name="block",
    )(*operands)
    return out[0], tuple(out[1:])


def body(images, dw_weight, dw_bias, ln_gain, ln_bias, w_in, b_in, w_out, b_out, layer_scale):
    segment = lax.axis_index("segment")
    sections = lax.axis_size("segment")
    place = lax.axis_index("dp")
    places = lax.axis_size("dp")
    micros, rows, width, channels = images.shape
    per_image = SIDE // rows
    half = per_image // 2
    even = place % 2 == 0

    others = [(p, p ^ 1) for p in range(places)]
    across = []
    for p in range(places):
        at = (p + half) % per_image
        if at == half - 1:
            across.append((p, (p + 1) % places))
        elif at == half:
            across.append((p, (p - 1) % places))

    def local_pairs(section, pairs):
        return [(section * places + a, section * places + b) for a, b in pairs]

    def next_pairs(section, pairs):
        return [(section * places + a, (section + 1) * places + b) for a, b in pairs]

    axes = ("segment", "dp")
    same = [(p, p) for p in range(places)]

    taps = jnp.where(even, dw_weight[0, ::-1], dw_weight[0]).reshape(TAPS * TAPS, 1, channels)
    taps = jnp.broadcast_to(taps, (TAPS * TAPS, 16, channels))
    select = np.zeros((width, TAPS * width), np.float32)
    for col in range(TAPS):
        for at in range(width):
            if 0 <= at + col - REACH < width:
                select[at, col * width + at + col - REACH] = 1
    params = (
        taps, dw_bias, ln_gain, ln_bias, jnp.asarray(select, BF), b_in, b_out, layer_scale,
    )
    weights = (w_in[0], w_out[0])

    mirror = even.astype(jnp.int32)
    flags = [jnp.stack([(segment == section).astype(jnp.int32), mirror]) for section in range(sections)]
    halos = []
    for m in range(micros):
        near, far, cross = mirrored_rows(flags[0], images[m])
        cross = lax.ppermute(cross, axes, local_pairs(0, across))
        swap = lax.ppermute(near, axes, local_pairs(0, others))
        halos.append((near, far, swap, cross))

    stash = None
    for section in range(sections):
        later = []
        for m in range(micros):
            near, far, swap, cross = halos[m]
            if section > 0:
                if m > 0:
                    near, stash = lax.optimization_barrier((near, stash))
                swap = lax.ppermute(near, axes, local_pairs(section, others))
            halo = (near, far, swap, cross)
            stash, (near, far, cross) = run_block(m, micros, flags[section], halo, params, weights, stash)
            if section < sections - 1:
                near = lax.ppermute(near, axes, next_pairs(section, same))
                cross = lax.ppermute(cross, axes, next_pairs(section, across))
                far = lax.ppermute(far, axes, next_pairs(section, same))
                later.append((near, far, None, cross))
        halos = later
    return stash


def solution(mesh):
    in_specs = (
        P(None, "dp", None, None),
        P("segment", None, None, None),
        P("segment", None),
        P("segment", None),
        P("segment", None),
        P("segment", None, None),
        P("segment", None),
        P("segment", None, None),
        P("segment", None),
        P("segment", None),
    )
    out_specs = P("segment", None, "dp", None, None)
    return jax.shard_map(body, mesh=mesh, in_specs=in_specs, out_specs=out_specs, check_vma=False)
```

```python
import functools

import jax
import jax.numpy as jnp
import numpy as np
from jax import lax
from jax.experimental import pallas as pl
from jax.experimental.pallas import tpu as pltpu
from jax.sharding import PartitionSpec as P

SIDE = 32
TAPS = 7
REACH = 3
NEAR = 3
LANES = 128
SUBLANES = 16
BF = jnp.bfloat16
F32 = jnp.float32
VECTORS = 5


def own_row(flip, rows, row):
    return flip * (rows - 1) + (1 - 2 * flip) * row


def run_copies(copies, sems):
    copies = [pltpu.make_async_copy(a, b, sems.at[i]) for i, (a, b) in enumerate(copies)]
    for copy in copies:
        copy.start()
    return copies


def rows_kernel(flags, images, *rest):
    micros, rows = images.shape[:2]
    sems = rest[-1]
    copies = []
    for m in range(micros):
        first, others, near, cross = rest[2 * m], rest[2 * m + 1], rest[2 * micros], rest[2 * micros + 1]
        for row in range(rows):
            here = images.at[m, own_row(flags[1], rows, row)]
            copies.append((here, first.at[row] if row < NEAR else others.at[row - NEAR]))
            if row < REACH:
                copies.append((here, near.at[m, row]))
            if row >= rows - REACH:
                copies.append((here, cross.at[m, row - (rows - REACH)]))
    for copy in run_copies(copies, sems):
        copy.wait()


def mirrored_rows(flags, images):
    micros, rows, width, channels = images.shape
    return pl.pallas_call(
        rows_kernel,
        out_shape=[pltpu.VMEM((NEAR, width, channels), BF), pltpu.VMEM((rows - NEAR, width, channels), BF)] * micros
        + [pltpu.VMEM((micros, REACH, width, channels), BF)] * 2,
        in_specs=[pl.BlockSpec(memory_space=pltpu.SMEM), pl.BlockSpec(memory_space=pltpu.HBM)],
        out_specs=[pl.BlockSpec(memory_space=pltpu.VMEM)] * (2 * micros + 2),
        scratch_shapes=[pltpu.SemaphoreType.DMA((micros * (rows + 2 * REACH),))],
        compiler_params=pltpu.CompilerParams(vmem_limit_bytes=2**20),
        cost_estimate=pl.CostEstimate(flops=0, bytes_accessed=2 * rows * width * channels, transcendentals=0),
        name="mirrored_rows",
    )(flags, pltpu.with_memory_space_constraint(images, pltpu.HBM))


def setup_kernel(flags, weight, conv_bias, gain, shift, b_out, scale, b_in, taps, vectors, inner, select, raw, sems):
    copies = [(v, vectors.at[i]) for i, v in enumerate((conv_bias, gain, shift, b_out, scale))]
    copies += [(b_in, inner)]
    copies += [(weight.at[0, jnp.where(flags[1] == 1, TAPS - 1 - i, i)], raw.at[i]) for i in range(TAPS)]
    copies = run_copies(copies, sems)
    width, depth = select.shape
    at = lax.broadcasted_iota(jnp.int32, (width, depth), 0)
    entry = lax.broadcasted_iota(jnp.int32, (width, depth), 1)
    hit = jnp.zeros((width, depth), jnp.bool_)
    for col in range(TAPS):
        hit = hit | ((entry - col * width == at + col - REACH) & (entry >= col * width) & (entry < (col + 1) * width))
    select[...] = hit.astype(F32).astype(BF)
    for copy in copies:
        copy.wait()
    for off in range(TAPS):
        rows = raw[off].astype(F32)
        for col in range(TAPS):
            one = jnp.broadcast_to(rows[col : col + 1, :], (SUBLANES, rows.shape[1]))
            taps[off * TAPS + col] = one.astype(BF)


def setup(flags, weight, vectors, b_in, width):
    channels = weight.shape[-1]
    operands = [pltpu.with_memory_space_constraint(v, pltpu.HBM) for v in (weight, *vectors, b_in)]
    return pl.pallas_call(
        setup_kernel,
        out_shape=[
            pltpu.VMEM((TAPS * TAPS, SUBLANES, channels), BF),
            pltpu.VMEM((VECTORS, 1, channels), F32),
            pltpu.VMEM(b_in.shape, F32),
            pltpu.VMEM((width, TAPS * width), BF),
        ],
        in_specs=[pl.BlockSpec(memory_space=pltpu.SMEM)] + [pl.BlockSpec(memory_space=pltpu.HBM)] * len(operands),
        out_specs=[pl.BlockSpec(memory_space=pltpu.VMEM)] * 4,
        scratch_shapes=[
            pltpu.VMEM((TAPS, TAPS, channels), BF),
            pltpu.SemaphoreType.DMA((VECTORS + 1 + TAPS,)),
        ],
        compiler_params=pltpu.CompilerParams(vmem_limit_bytes=4 * 2**20),
        cost_estimate=pl.CostEstimate(flops=0, bytes_accessed=2**22, transcendentals=0),
        name="setup",
    )(flags, *operands)


def block_kernel(micro, last, final, chunk, *refs):
    refs = list(refs)
    flags, near, far, swap, cross, taps, vectors, inner_bias, select, w_in_hbm, w_out_hbm = refs[:11]
    w_in, w_out, sums, normal, total, *tail = refs[-7 if last else -6 :]
    sems = tail[-1]
    outs = refs[11 : -7 if last else -6]
    if last:
        earlier, stash, result = outs[0], outs[-1], tail[0]
    else:
        result = outs[-1]
    near_out, far_out, cross_out = (None, None, None) if final else outs[-4:-1]
    rows, width, channels = near.shape[0] + far.shape[0], near.shape[1], near.shape[2]
    swap = swap.at[micro] if len(swap.shape) == 4 else swap
    cross = cross.at[micro] if len(cross.shape) == 4 else cross
    hidden = w_in.shape[1]
    conv_bias, gain, shift, b_out, scale = (vectors.at[i] for i in range(VECTORS))

    def own(row):
        return near.at[row] if row < NEAR else far.at[row - NEAR]

    def source(row, lanes):
        if row < REACH:
            return swap[REACH - 1 - row, :, lanes]
        if row < REACH + rows:
            return own(row - REACH)[:, lanes]
        return cross[2 * REACH + rows - 1 - row, :, lanes]

    @pl.when(flags[0] == 1)
    def _():
        get_in = pltpu.make_async_copy(w_in_hbm, w_in, sems.at[0])
        get_out = pltpu.make_async_copy(w_out_hbm, w_out, sems.at[1])
        get_in.start()
        get_out.start()
        if last:
            keep_earlier = pltpu.make_async_copy(earlier, stash.at[0, micro - 1], sems.at[2])
            keep_earlier.start()
        for group in range(channels // LANES):
            lanes = slice(group * LANES, (group + 1) * LANES)
            inputs = [source(row, lanes) for row in range(rows + 2 * REACH)]
            for col in range(TAPS):
                parts = [None] * rows
                for off in range(TAPS):
                    tap = taps[off * TAPS + col, :, lanes]
                    tap = jnp.concatenate([tap] * (width // SUBLANES), axis=0)
                    for row in range(rows):
                        term = inputs[row + off] * tap
                        parts[row] = term if off == 0 else parts[row] + term
                for row in range(rows):
                    sums[row, col * width : (col + 1) * width, lanes] = parts[row]
        for row in range(rows):
            conv = jnp.dot(select[...], sums[row], preferred_element_type=F32) + conv_bias[...]
            centred = conv - jnp.mean(conv, axis=-1, keepdims=True)
            var = jnp.mean(centred * centred, axis=-1, keepdims=True)
            here = slice(row * width, (row + 1) * width)
            normal[here, :] = (centred * lax.rsqrt(var + 1e-06) * gain[...] + shift[...]).astype(BF)
        get_in.wait()
        for start in range(0, hidden, chunk):
            part = slice(start, start + chunk)
            inner = jnp.dot(normal[...], w_in[:, part], preferred_element_type=F32) + inner_bias[:, part]
            act = (0.5 * inner * (1.0 + lax.erf(inner * np.float32(0.5**0.5)))).astype(BF)
            if start == 0:
                get_out.wait()
            branch = jnp.dot(act, w_out[part, :], preferred_element_type=F32)
            if start == 0:
                total[...] = branch
            else:
                total[...] += branch
        for row in range(rows):
            branch = total[row * width : (row + 1) * width, :] + b_out[...]
            value = (own(row)[...].astype(F32) + scale[...] * branch).astype(BF)
            if not final:
                if row < NEAR:
                    near_out[row] = value
                else:
                    far_out[row - NEAR] = value
                if row >= rows - REACH:
                    cross_out[row - (rows - REACH)] = value
            result[own_row(flags[1], rows, row)] = value
        if last:
            keep = pltpu.make_async_copy(result, stash.at[0, micro], sems.at[3])
            keep.start()
            keep_earlier.wait()
            keep.wait()


def run_block(micro, micros, final, flags, halo, params, weights, earlier, stash):
    last = micro == micros - 1
    near, far = halo[:2]
    rows, width, channels = near.shape[0] + far.shape[0], near.shape[1], near.shape[2]
    vmem = pl.BlockSpec(memory_space=pltpu.VMEM)
    anywhere = pl.BlockSpec(memory_space=pl.ANY)
    held = [pltpu.with_memory_space_constraint(v, pltpu.VMEM) for v in [*halo, *params]]
    pinned = [pltpu.with_memory_space_constraint(v, pltpu.HBM) for v in weights]
    operands = [flags] + held + pinned
    specs = [pl.BlockSpec(memory_space=pltpu.SMEM)] + [vmem] * len(held)
    specs += [pl.BlockSpec(memory_space=pltpu.HBM)] * len(pinned)
    counts = () if final else (NEAR, rows - NEAR, REACH)
    out_shape = [pltpu.VMEM((count, width, channels), BF) for count in counts]
    scratch = [
        pltpu.VMEM(weights[0].shape, BF),
        pltpu.VMEM(weights[1].shape, BF),
        pltpu.VMEM((rows, TAPS * width, channels), BF),
        pltpu.VMEM((rows * width, channels), BF),
        pltpu.VMEM((rows * width, channels), F32),
    ]
    result = pltpu.VMEM((rows, width, channels), BF)
    out_specs = [vmem] * len(out_shape)
    aliases = {}
    if last:
        operands.append(pltpu.with_memory_space_constraint(earlier, pltpu.VMEM))
        specs.append(vmem)
        if stash is not None:
            aliases = {len(operands): len(out_shape)}
            operands.append(stash)
            specs.append(anywhere)
        out_shape.append(jax.ShapeDtypeStruct((1, micros, rows, width, channels), BF))
        out_specs.append(anywhere)
        scratch.append(result)
    else:
        out_shape.append(result)
        out_specs.append(vmem)
    *relayed, kept = pl.pallas_call(
        functools.partial(block_kernel, micro, last, final, 768),
        out_shape=out_shape,
        in_specs=specs,
        out_specs=out_specs,
        scratch_shapes=scratch + [pltpu.SemaphoreType.DMA((4,))],
        input_output_aliases=aliases,
        compiler_params=pltpu.CompilerParams(vmem_limit_bytes=32 * 2**20),
        cost_estimate=pl.CostEstimate(flops=2**20, bytes_accessed=2**10, transcendentals=0),
        name="block",
    )(*operands)
    return relayed, kept


def body(images, dw_weight, dw_bias, ln_gain, ln_bias, w_in, b_in, w_out, b_out, layer_scale):
    segment = lax.axis_index("segment")
    sections = lax.axis_size("segment")
    place = lax.axis_index("dp")
    places = lax.axis_size("dp")
    micros, rows, width, channels = images.shape
    per_image = SIDE // rows
    half = per_image // 2
    reverse = (place % 2 == 0).astype(jnp.int32)
    flags = [jnp.stack([(segment == section).astype(jnp.int32), reverse]) for section in range(sections)]

    axes = ("segment", "dp")

    def index(section, p):
        return section % sections * places + p % places

    facing = {}
    for p in range(places):
        if (p + half) % per_image in (half - 1, half):
            facing[p] = p + 1 if p % 2 == 1 else p - 1
    swap_pairs = [(index(s, p), index(s, p ^ 1)) for s in range(sections) for p in range(places)]
    near_pairs = [(index(s, p), index(s, q)) for s in range(sections) for p, q in facing.items()]

    def relay_pairs(section, onward):
        idle = [(index(section + 2, p), index(section, p)) for p in range(places)]
        return [(index(section, p), index(section + 1, q)) for p, q in onward.items()] + idle

    same = {p: p for p in range(places)}

    *wholes, near, cross = mirrored_rows(flags[0], images)
    cross = lax.ppermute(cross, axes, near_pairs)
    swap = lax.ppermute(near, axes, swap_pairs)
    params = setup(flags[0], dw_weight, (dw_bias, ln_gain, ln_bias, b_out, layer_scale), b_in, width)
    weights = (w_in[0], w_out[0])

    halos = [(wholes[2 * m], wholes[2 * m + 1], swap, cross) for m in range(micros)]
    stash = before = None
    for section in range(sections):
        later, earlier = [], None
        for m in range(micros):
            near, far, swap, cross = halos[m]
            if section > 0:
                near, _ = lax.optimization_barrier((near, before))
                swap = lax.ppermute(near, axes, swap_pairs)
            halo = (near, far, swap, cross)
            final = section == sections - 1
            relayed, kept = run_block(m, micros, final, flags[section], halo, params, weights, earlier, stash)
            before = kept
            if m == micros - 1:
                stash = kept
            else:
                earlier = kept
            if not final:
                near, far = (lax.ppermute(v, axes, relay_pairs(section, same)) for v in relayed[:2])
                cross = lax.ppermute(relayed[2], axes, relay_pairs(section, facing))
                later.append((near, far, None, cross))
        halos = later
    return stash


def solution(mesh):
    in_specs = (
        P(None, "dp", None, None),
        P("segment", None, None, None),
        P("segment", None),
        P("segment", None),
        P("segment", None),
        P("segment", None, None),
        P("segment", None),
        P("segment", None, None),
        P("segment", None),
        P("segment", None),
    )
    out_specs = P("segment", None, "dp", None, None)
    return jax.shard_map(body, mesh=mesh, in_specs=in_specs, out_specs=out_specs, check_vma=False)
```

```python
import functools

import jax
import jax.numpy as jnp
import numpy as np
from jax import lax
from jax.experimental import pallas as pl
from jax.experimental.pallas import tpu as pltpu
from jax.sharding import PartitionSpec as P

SIDE = 32
TAPS = 7
REACH = 3
CROSS = 5
LANES = 128
SUBLANES = 16
BF = jnp.bfloat16
F32 = jnp.float32
VECTORS = 5


def own_row(flip, rows, row):
    return flip * (rows - 1) + (1 - 2 * flip) * row


def run_copies(copies, sems):
    copies = [pltpu.make_async_copy(a, b, sems.at[i]) for i, (a, b) in enumerate(copies)]
    for copy in copies:
        copy.start()
    return copies


def rows_kernel(flags, images, *rest):
    micros, rows = images.shape[:2]
    sems = rest[-1]
    copies = []
    for m in range(micros):
        whole, near, cross = rest[m], rest[micros], rest[micros + 1]
        for row in range(rows):
            here = images.at[m, own_row(flags[1], rows, row)]
            copies.append((here, whole.at[row]))
            if row < REACH:
                copies.append((here, near.at[m, row]))
            if row >= rows - CROSS:
                copies.append((here, cross.at[m, row - (rows - CROSS)]))
    for copy in run_copies(copies, sems):
        copy.wait()


def mirrored_rows(flags, images):
    micros, rows, width, channels = images.shape
    return pl.pallas_call(
        rows_kernel,
        out_shape=[pltpu.VMEM((rows, width, channels), BF)] * micros
        + [pltpu.VMEM((micros, count, width, channels), BF) for count in (REACH, CROSS)],
        in_specs=[pl.BlockSpec(memory_space=pltpu.SMEM), pl.BlockSpec(memory_space=pltpu.HBM)],
        out_specs=[pl.BlockSpec(memory_space=pltpu.VMEM)] * (micros + 2),
        scratch_shapes=[pltpu.SemaphoreType.DMA((micros * (rows + REACH + CROSS),))],
        compiler_params=pltpu.CompilerParams(vmem_limit_bytes=2**20),
        cost_estimate=pl.CostEstimate(flops=0, bytes_accessed=2 * rows * width * channels, transcendentals=0),
        name="mirrored_rows",
    )(flags, pltpu.with_memory_space_constraint(images, pltpu.HBM))


def setup_kernel(flags, weight, conv_bias, gain, shift, b_out, scale, b_in, taps, vectors, inner, select, raw, sems):
    copies = [(v, vectors.at[i]) for i, v in enumerate((conv_bias, gain, shift, b_out, scale))]
    copies += [(b_in, inner)]
    copies += [(weight.at[0, jnp.where(flags[1] == 1, TAPS - 1 - i, i)], raw.at[i]) for i in range(TAPS)]
    copies = run_copies(copies, sems)
    width, depth = select.shape
    at = lax.broadcasted_iota(jnp.int32, (width, depth), 0)
    entry = lax.broadcasted_iota(jnp.int32, (width, depth), 1)
    hit = jnp.zeros((width, depth), jnp.bool_)
    for col in range(TAPS):
        hit = hit | ((entry - col * width == at + col - REACH) & (entry >= col * width) & (entry < (col + 1) * width))
    select[...] = hit.astype(F32).astype(BF)
    for copy in copies:
        copy.wait()
    for off in range(TAPS):
        rows = raw[off].astype(F32)
        for col in range(TAPS):
            one = jnp.broadcast_to(rows[col : col + 1, :], (SUBLANES, rows.shape[1]))
            taps[off * TAPS + col] = one.astype(BF)


def setup(flags, weight, vectors, b_in, width):
    channels = weight.shape[-1]
    operands = [pltpu.with_memory_space_constraint(v, pltpu.HBM) for v in (weight, *vectors, b_in)]
    return pl.pallas_call(
        setup_kernel,
        out_shape=[
            pltpu.VMEM((TAPS * TAPS, SUBLANES, channels), BF),
            pltpu.VMEM((VECTORS, 1, channels), F32),
            pltpu.VMEM(b_in.shape, F32),
            pltpu.VMEM((width, TAPS * width), BF),
        ],
        in_specs=[pl.BlockSpec(memory_space=pltpu.SMEM)] + [pl.BlockSpec(memory_space=pltpu.HBM)] * len(operands),
        out_specs=[pl.BlockSpec(memory_space=pltpu.VMEM)] * 4,
        scratch_shapes=[
            pltpu.VMEM((TAPS, TAPS, channels), BF),
            pltpu.SemaphoreType.DMA((VECTORS + 1 + TAPS,)),
        ],
        compiler_params=pltpu.CompilerParams(vmem_limit_bytes=4 * 2**20),
        cost_estimate=pl.CostEstimate(flops=0, bytes_accessed=2**22, transcendentals=0),
        name="setup",
    )(flags, *operands)


def block_kernel(micro, last, final, chunk, *refs):
    refs = list(refs)
    flags, whole, swap, cross, taps, vectors, inner_bias, select, w_in_hbm, w_out_hbm = refs[:10]
    w_in, w_out, sums, normal, total, *tail = refs[-7 if last else -6 :]
    sems = tail[-1]
    outs = refs[10 : -7 if last else -6]
    if last:
        earlier, stash, result = outs[0], outs[-1], tail[0]
    else:
        result = outs[-1]
    whole_out, cross_out = (None, None) if final else outs[-3:-1]
    rows, width, channels = whole.shape
    swap = swap.at[micro] if len(swap.shape) == 4 else swap
    cross = cross.at[micro] if len(cross.shape) == 4 else cross
    hidden = w_in.shape[1]
    conv_bias, gain, shift, b_out, scale = (vectors.at[i] for i in range(VECTORS))

    def source(row, lanes):
        if row < REACH:
            return swap[REACH - 1 - row, :, lanes]
        if row < REACH + rows:
            return whole[row - REACH, :, lanes]
        return cross[REACH + CROSS + rows - 1 - row, :, lanes]

    @pl.when(flags[0] == 1)
    def _():
        get_in = pltpu.make_async_copy(w_in_hbm, w_in, sems.at[0])
        get_out = pltpu.make_async_copy(w_out_hbm, w_out, sems.at[1])
        get_in.start()
        get_out.start()
        if last:
            keep_earlier = pltpu.make_async_copy(earlier, stash.at[0, micro - 1], sems.at[2])
            keep_earlier.start()
        for group in range(channels // LANES):
            lanes = slice(group * LANES, (group + 1) * LANES)
            inputs = [source(row, lanes) for row in range(rows + 2 * REACH)]
            for col in range(TAPS):
                parts = [None] * rows
                for off in range(TAPS):
                    tap = taps[off * TAPS + col, :, lanes]
                    tap = jnp.concatenate([tap] * (width // SUBLANES), axis=0)
                    for row in range(rows):
                        term = inputs[row + off] * tap
                        parts[row] = term if off == 0 else parts[row] + term
                for row in range(rows):
                    sums[row, col * width : (col + 1) * width, lanes] = parts[row]
        for row in range(rows):
            conv = jnp.dot(select[...], sums[row], preferred_element_type=F32) + conv_bias[...]
            centred = conv - jnp.mean(conv, axis=-1, keepdims=True)
            var = jnp.mean(centred * centred, axis=-1, keepdims=True)
            here = slice(row * width, (row + 1) * width)
            normal[here, :] = (centred * lax.rsqrt(var + 1e-06) * gain[...] + shift[...]).astype(BF)
        get_in.wait()
        for start in range(0, hidden, chunk):
            part = slice(start, start + chunk)
            inner = jnp.dot(normal[...], w_in[:, part], preferred_element_type=F32) + inner_bias[:, part]
            act = (0.5 * inner * (1.0 + lax.erf(inner * np.float32(0.5**0.5)))).astype(BF)
            if start == 0:
                get_out.wait()
            branch = jnp.dot(act, w_out[part, :], preferred_element_type=F32)
            if start == 0:
                total[...] = branch
            else:
                total[...] += branch
        for row in range(rows):
            branch = total[row * width : (row + 1) * width, :] + b_out[...]
            value = (whole[row].astype(F32) + scale[...] * branch).astype(BF)
            if not final:
                whole_out[row] = value
                if row >= rows - CROSS:
                    cross_out[row - (rows - CROSS)] = value
            result[own_row(flags[1], rows, row)] = value
        if last:
            keep = pltpu.make_async_copy(result, stash.at[0, micro], sems.at[3])
            keep.start()
            keep_earlier.wait()
            keep.wait()


def run_block(micro, micros, final, flags, halo, params, weights, earlier, stash):
    last = micro == micros - 1
    rows, width, channels = halo[0].shape
    vmem = pl.BlockSpec(memory_space=pltpu.VMEM)
    anywhere = pl.BlockSpec(memory_space=pl.ANY)
    held = [pltpu.with_memory_space_constraint(v, pltpu.VMEM) for v in [*halo, *params]]
    pinned = [pltpu.with_memory_space_constraint(v, pltpu.HBM) for v in weights]
    operands = [flags] + held + pinned
    specs = [pl.BlockSpec(memory_space=pltpu.SMEM)] + [vmem] * len(held)
    specs += [pl.BlockSpec(memory_space=pltpu.HBM)] * len(pinned)
    counts = () if final else (rows, CROSS)
    out_shape = [pltpu.VMEM((count, width, channels), BF) for count in counts]
    scratch = [
        pltpu.VMEM(weights[0].shape, BF),
        pltpu.VMEM(weights[1].shape, BF),
        pltpu.VMEM((rows, TAPS * width, channels), BF),
        pltpu.VMEM((rows * width, channels), BF),
        pltpu.VMEM((rows * width, channels), F32),
    ]
    result = pltpu.VMEM((rows, width, channels), BF)
    out_specs = [vmem] * len(out_shape)
    aliases = {}
    if last:
        operands.append(pltpu.with_memory_space_constraint(earlier, pltpu.VMEM))
        specs.append(vmem)
        if stash is not None:
            aliases = {len(operands): len(out_shape)}
            operands.append(stash)
            specs.append(anywhere)
        out_shape.append(jax.ShapeDtypeStruct((1, micros, rows, width, channels), BF))
        out_specs.append(anywhere)
        scratch.append(result)
    else:
        out_shape.append(result)
        out_specs.append(vmem)
    *relayed, kept = pl.pallas_call(
        functools.partial(block_kernel, micro, last, final, 768),
        out_shape=out_shape,
        in_specs=specs,
        out_specs=out_specs,
        scratch_shapes=scratch + [pltpu.SemaphoreType.DMA((4,))],
        input_output_aliases=aliases,
        compiler_params=pltpu.CompilerParams(vmem_limit_bytes=32 * 2**20),
        cost_estimate=pl.CostEstimate(flops=2**20 if last else 2**33, bytes_accessed=2**10, transcendentals=0),
        name="block",
    )(*operands)
    return relayed, kept


def body(images, dw_weight, dw_bias, ln_gain, ln_bias, w_in, b_in, w_out, b_out, layer_scale):
    segment = lax.axis_index("segment")
    sections = lax.axis_size("segment")
    place = lax.axis_index("dp")
    places = lax.axis_size("dp")
    micros, rows, width, channels = images.shape
    per_image = SIDE // rows
    half = per_image // 2
    reverse = (place % 2 == 0).astype(jnp.int32)
    flags = [jnp.stack([(segment == section).astype(jnp.int32), reverse]) for section in range(sections)]

    axes = ("segment", "dp")

    def index(section, p):
        return section % sections * places + p % places

    facing = {}
    for p in range(places):
        if (p + half) % per_image in (half - 1, half):
            facing[p] = p + 1 if p % 2 == 1 else p - 1
    swap_pairs = [(index(s, p), index(s, p ^ 1)) for s in range(sections) for p in range(places)]
    near_pairs = [(index(s, p), index(s, q)) for s in range(sections) for p, q in facing.items()]

    def relay_pairs(section, onward):
        return [(index(section, p), index(section + 1, q)) for p, q in onward.items()]

    same = {p: p for p in range(places)}

    *wholes, near, cross = mirrored_rows(flags[0], images)
    cross = lax.ppermute(cross, axes, near_pairs)
    swap = lax.ppermute(near, axes, swap_pairs)
    params = setup(flags[0], dw_weight, (dw_bias, ln_gain, ln_bias, b_out, layer_scale), b_in, width)
    weights = (w_in[0], w_out[0])

    halos = [(wholes[m], swap, cross) for m in range(micros)]
    stash = before = None
    for section in range(sections):
        later, earlier = [], None
        for m in range(micros):
            whole, swap, cross = halos[m]
            if section > 0:
                whole, cross, _ = lax.optimization_barrier((whole, cross, before))
                swap = lax.ppermute(whole[:REACH], axes, swap_pairs)
            halo = (whole, swap, cross)
            final = section == sections - 1
            relayed, kept = run_block(m, micros, final, flags[section], halo, params, weights, earlier, stash)
            before = kept
            if m == micros - 1:
                stash = kept
            else:
                earlier = kept
            if not final:
                whole = lax.ppermute(relayed[0], axes, relay_pairs(section, same))
                cross = lax.ppermute(relayed[1], axes, relay_pairs(section, facing))
                later.append((whole, None, cross))
        halos = later
    return stash


def solution(mesh):
    in_specs = (
        P(None, "dp", None, None),
        P("segment", None, None, None),
        P("segment", None),
        P("segment", None),
        P("segment", None),
        P("segment", None, None),
        P("segment", None),
        P("segment", None, None),
        P("segment", None),
        P("segment", None),
    )
    out_specs = P("segment", None, "dp", None, None)
    return jax.shard_map(body, mesh=mesh, in_specs=in_specs, out_specs=out_specs, check_vma=False)
```

```python
import functools

import jax
import jax.numpy as jnp
import numpy as np
from jax import lax
from jax.experimental import pallas as pl
from jax.experimental.pallas import tpu as pltpu
from jax.sharding import PartitionSpec as P

SIDE = 32
TAPS = 7
REACH = 3
CROSS = 3
NEAR = 3
LANES = 128
SUBLANES = 16
BF = jnp.bfloat16
F32 = jnp.float32
VECTORS = 5


def own_row(flip, rows, row):
    return flip * (rows - 1) + (1 - 2 * flip) * row


def run_copies(copies, sems):
    copies = [pltpu.make_async_copy(a, b, sems.at[i]) for i, (a, b) in enumerate(copies)]
    for copy in copies:
        copy.start()
    return copies


def rows_kernel(flags, images, *rest):
    micros, rows = images.shape[:2]
    sems = rest[-1]
    copies = []
    for m in range(micros):
        near, far, cross = rest[m], rest[micros + m], rest[2 * micros]
        for row in range(rows):
            here = images.at[m, own_row(flags[1], rows, row)]
            copies.append((here, near.at[row] if row < NEAR else far.at[row - NEAR]))
            if row >= rows - CROSS:
                copies.append((here, cross.at[m, row - (rows - CROSS)]))
    for copy in run_copies(copies, sems):
        copy.wait()


def mirrored_rows(flags, images):
    micros, rows, width, channels = images.shape
    return pl.pallas_call(
        rows_kernel,
        out_shape=[pltpu.VMEM((NEAR, width, channels), BF)] * micros
        + [pltpu.VMEM((rows - NEAR, width, channels), BF)] * micros
        + [pltpu.VMEM((micros, CROSS, width, channels), BF)],
        in_specs=[pl.BlockSpec(memory_space=pltpu.SMEM), pl.BlockSpec(memory_space=pltpu.HBM)],
        out_specs=[pl.BlockSpec(memory_space=pltpu.VMEM)] * (2 * micros + 1),
        scratch_shapes=[pltpu.SemaphoreType.DMA((micros * (rows + CROSS),))],
        compiler_params=pltpu.CompilerParams(vmem_limit_bytes=2**20),
        cost_estimate=pl.CostEstimate(flops=0, bytes_accessed=2 * rows * width * channels, transcendentals=0),
        name="mirrored_rows",
    )(flags, pltpu.with_memory_space_constraint(images, pltpu.HBM))


def setup_kernel(flags, weight, conv_bias, gain, shift, b_out, scale, b_in, taps, vectors, inner, select, raw, sems):
    copies = [(v, vectors.at[i]) for i, v in enumerate((conv_bias, gain, shift, b_out, scale))]
    copies += [(b_in, inner)]
    copies += [(weight.at[0, jnp.where(flags[1] == 1, TAPS - 1 - i, i)], raw.at[i]) for i in range(TAPS)]
    copies = run_copies(copies, sems)
    width, depth = select.shape
    at = lax.broadcasted_iota(jnp.int32, (width, depth), 0)
    entry = lax.broadcasted_iota(jnp.int32, (width, depth), 1)
    hit = jnp.zeros((width, depth), jnp.bool_)
    for col in range(TAPS):
        hit = hit | ((entry - col * width == at + col - REACH) & (entry >= col * width) & (entry < (col + 1) * width))
    select[...] = hit.astype(F32).astype(BF)
    for copy in copies:
        copy.wait()
    for off in range(TAPS):
        rows = raw[off].astype(F32)
        for col in range(TAPS):
            one = jnp.broadcast_to(rows[col : col + 1, :], (SUBLANES, rows.shape[1]))
            taps[off * TAPS + col] = one.astype(BF)


def setup(flags, weight, vectors, b_in, width):
    channels = weight.shape[-1]
    operands = [pltpu.with_memory_space_constraint(v, pltpu.HBM) for v in (weight, *vectors, b_in)]
    return pl.pallas_call(
        setup_kernel,
        out_shape=[
            pltpu.VMEM((TAPS * TAPS, SUBLANES, channels), BF),
            pltpu.VMEM((VECTORS, 1, channels), F32),
            pltpu.VMEM(b_in.shape, F32),
            pltpu.VMEM((width, TAPS * width), BF),
        ],
        in_specs=[pl.BlockSpec(memory_space=pltpu.SMEM)] + [pl.BlockSpec(memory_space=pltpu.HBM)] * len(operands),
        out_specs=[pl.BlockSpec(memory_space=pltpu.VMEM)] * 4,
        scratch_shapes=[
            pltpu.VMEM((TAPS, TAPS, channels), BF),
            pltpu.SemaphoreType.DMA((VECTORS + 1 + TAPS,)),
        ],
        compiler_params=pltpu.CompilerParams(vmem_limit_bytes=4 * 2**20),
        cost_estimate=pl.CostEstimate(flops=0, bytes_accessed=2**22, transcendentals=0),
        name="setup",
    )(flags, *operands)


def block_kernel(micro, last, final, chunk, *refs):
    refs = list(refs)
    flags, near, far, swap, cross, taps, vectors, inner_bias, select, w_in_hbm, w_out_hbm = refs[:11]
    w_in, w_out, sums, normal, total, *tail = refs[-7 if last else -6 :]
    sems = tail[-1]
    outs = refs[11 : -7 if last else -6]
    if last:
        earlier, stash, result = outs[0], outs[-1], tail[0]
    else:
        result = outs[-1]
    near_out, far_out, cross_out = (None, None, None) if final else outs[-4:-1]
    rows, width, channels = near.shape[0] + far.shape[0], near.shape[1], near.shape[2]
    cross = cross.at[micro] if len(cross.shape) == 4 else cross
    hidden = w_in.shape[1]
    conv_bias, gain, shift, b_out, scale = (vectors.at[i] for i in range(VECTORS))

    def source(row, lanes):
        if row < REACH:
            return swap[REACH - 1 - row, :, lanes]
        if row < REACH + NEAR:
            return near[row - REACH, :, lanes]
        if row < REACH + rows:
            return far[row - REACH - NEAR, :, lanes]
        return cross[REACH + CROSS + rows - 1 - row, :, lanes]

    @pl.when(flags[0] == 1)
    def _():
        get_in = pltpu.make_async_copy(w_in_hbm, w_in, sems.at[0])
        get_out = pltpu.make_async_copy(w_out_hbm, w_out, sems.at[1])
        get_in.start()
        get_out.start()
        if last:
            keep_earlier = pltpu.make_async_copy(earlier, stash.at[0, micro - 1], sems.at[2])
            keep_earlier.start()
        @pl.loop(0, channels // LANES)
        def _(group):
            lanes = pl.ds(pl.multiple_of(group * LANES, LANES), LANES)
            inputs = [source(row, lanes) for row in range(rows + 2 * REACH)]
            for col in range(TAPS):
                parts = [None] * rows
                for off in range(TAPS):
                    tap = taps[off * TAPS + col, :, lanes]
                    tap = jnp.concatenate([tap] * (width // SUBLANES), axis=0)
                    for row in range(rows):
                        term = inputs[row + off] * tap
                        parts[row] = term if off == 0 else parts[row] + term
                for row in range(rows):
                    sums[row, col * width : (col + 1) * width, lanes] = parts[row]

        @pl.loop(0, rows, unroll=2)
        def _(row):
            conv = jnp.dot(select[...], sums[row], preferred_element_type=F32) + conv_bias[...]
            centred = conv - jnp.mean(conv, axis=-1, keepdims=True)
            var = jnp.mean(centred * centred, axis=-1, keepdims=True)
            normed = (centred * lax.rsqrt(var + 1e-06) * gain[...] + shift[...]).astype(BF)
            normal[pl.ds(pl.multiple_of(row * width, width), width), :] = normed

        get_in.wait()
        for start in range(0, hidden, chunk):
            part = slice(start, start + chunk)
            inner = jnp.dot(normal[...], w_in[:, part], preferred_element_type=F32) + inner_bias[:, part]
            act = (0.5 * inner * (1.0 + lax.erf(inner * np.float32(0.5**0.5)))).astype(BF)
            if start == 0:
                get_out.wait()
            branch = jnp.dot(act, w_out[part, :], preferred_element_type=F32)
            if start == 0:
                total[...] = branch
            else:
                total[...] += branch
        def outcome(row, value):
            branch = total[pl.ds(pl.multiple_of(row * width, width), width), :] + b_out[...]
            value = (value.astype(F32) + scale[...] * branch).astype(BF)
            result[own_row(flags[1], rows, row)] = value
            return value

        @pl.loop(0, NEAR)
        def _(row):
            value = outcome(row, near[row])
            if not final:
                near_out[row] = value

        @pl.loop(0, rows - NEAR)
        def _(row):
            value = outcome(row + NEAR, far[row])
            if not final:
                far_out[row] = value
                if rows - NEAR == CROSS:
                    cross_out[row] = value
                else:

                    @pl.when(row >= rows - NEAR - CROSS)
                    def _():
                        cross_out[jnp.maximum(row - (rows - NEAR - CROSS), 0)] = value

        if last:
            keep = pltpu.make_async_copy(result, stash.at[0, micro], sems.at[3])
            keep.start()
            keep_earlier.wait()
            keep.wait()


def run_block(micro, micros, final, flags, halo, params, weights, earlier, stash):
    last = micro == micros - 1
    near, far = halo[:2]
    rows, width, channels = near.shape[0] + far.shape[0], near.shape[1], near.shape[2]
    vmem = pl.BlockSpec(memory_space=pltpu.VMEM)
    anywhere = pl.BlockSpec(memory_space=pl.ANY)
    held = [pltpu.with_memory_space_constraint(v, pltpu.VMEM) for v in [*halo, *params]]
    pinned = [pltpu.with_memory_space_constraint(v, pltpu.HBM) for v in weights]
    operands = [flags] + held + pinned
    specs = [pl.BlockSpec(memory_space=pltpu.SMEM)] + [vmem] * len(held)
    specs += [pl.BlockSpec(memory_space=pltpu.HBM)] * len(pinned)
    counts = () if final else (NEAR, rows - NEAR, CROSS)
    out_shape = [pltpu.VMEM((count, width, channels), BF) for count in counts]
    scratch = [
        pltpu.VMEM(weights[0].shape, BF),
        pltpu.VMEM(weights[1].shape, BF),
        pltpu.VMEM((rows, TAPS * width, channels), BF),
        pltpu.VMEM((rows * width, channels), BF),
        pltpu.VMEM((rows * width, channels), F32),
    ]
    result = pltpu.VMEM((rows, width, channels), BF)
    out_specs = [vmem] * len(out_shape)
    aliases = {}
    if last:
        operands.append(pltpu.with_memory_space_constraint(earlier, pltpu.VMEM))
        specs.append(vmem)
        if stash is not None:
            aliases = {len(operands): len(out_shape)}
            operands.append(stash)
            specs.append(anywhere)
        out_shape.append(jax.ShapeDtypeStruct((1, micros, rows, width, channels), BF))
        out_specs.append(anywhere)
        scratch.append(result)
    else:
        out_shape.append(result)
        out_specs.append(vmem)
    *relayed, kept = pl.pallas_call(
        functools.partial(block_kernel, micro, last, final, 768),
        out_shape=out_shape,
        in_specs=specs,
        out_specs=out_specs,
        scratch_shapes=scratch + [pltpu.SemaphoreType.DMA((4,))],
        input_output_aliases=aliases,
        compiler_params=pltpu.CompilerParams(vmem_limit_bytes=32 * 2**20),
        cost_estimate=pl.CostEstimate(flops=2**33 if last else 2**33, bytes_accessed=2**10, transcendentals=0),
        name="block",
    )(*operands)
    return relayed, kept


def body(images, dw_weight, dw_bias, ln_gain, ln_bias, w_in, b_in, w_out, b_out, layer_scale):
    segment = lax.axis_index("segment")
    sections = lax.axis_size("segment")
    place = lax.axis_index("dp")
    places = lax.axis_size("dp")
    micros, rows, width, channels = images.shape
    per_image = SIDE // rows
    half = per_image // 2
    reverse = (place % 2 == 0).astype(jnp.int32)
    flags = [jnp.stack([(segment == section).astype(jnp.int32), reverse]) for section in range(sections)]

    axes = ("segment", "dp")

    def index(section, p):
        return section % sections * places + p % places

    facing = {}
    for p in range(places):
        if (p + half) % per_image in (half - 1, half):
            facing[p] = p + 1 if p % 2 == 1 else p - 1
    swap_pairs = [(index(s, p), index(s, p ^ 1)) for s in range(sections) for p in range(places)]
    near_pairs = [(index(s, p), index(s, q)) for s in range(sections) for p, q in facing.items()]

    def relay_pairs(section, onward):
        return [(index(section, p), index(section + 1, q)) for p, q in onward.items()]

    same = {p: p for p in range(places)}

    *parts, cross = mirrored_rows(flags[0], images)
    cross = lax.ppermute(cross, axes, near_pairs)
    params = setup(flags[0], dw_weight, (dw_bias, ln_gain, ln_bias, b_out, layer_scale), b_in, width)
    weights = (w_in[0], w_out[0])

    halos = [(parts[m], parts[micros + m], cross) for m in range(micros)]
    stash = before = None
    for section in range(sections):
        later, earlier = [], None
        for m in range(micros):
            near, far, cross = halos[m]
            if section > 0:
                near, _ = lax.optimization_barrier((near, before))
            swap = lax.ppermute(near, axes, swap_pairs)
            halo = (near, far, swap, cross)
            final = section == sections - 1
            relayed, kept = run_block(m, micros, final, flags[section], halo, params, weights, earlier, stash)
            before = kept
            if m == micros - 1:
                stash = kept
            else:
                earlier = kept
            if not final:
                near = lax.ppermute(relayed[0], axes, relay_pairs(section, same))
                cross = lax.ppermute(relayed[2], axes, relay_pairs(section, facing))
                far = lax.ppermute(relayed[1], axes, relay_pairs(section, same))
                later.append((near, far, cross))
        halos = later
    return stash


def solution(mesh):
    in_specs = (
        P(None, "dp", None, None),
        P("segment", None, None, None),
        P("segment", None),
        P("segment", None),
        P("segment", None),
        P("segment", None, None),
        P("segment", None),
        P("segment", None, None),
        P("segment", None),
        P("segment", None),
    )
    out_specs = P("segment", None, "dp", None, None)
    return jax.shard_map(body, mesh=mesh, in_specs=in_specs, out_specs=out_specs, check_vma=False)
```

```python
import functools

import jax
import jax.numpy as jnp
import numpy as np
from jax import lax
from jax.experimental import pallas as pl
from jax.experimental.pallas import tpu as pltpu
from jax.sharding import PartitionSpec as P

SIDE = 32
TAPS = 7
REACH = 3
CROSS = 3
NEAR = 3
LANES = 128
SUBLANES = 16
BF = jnp.bfloat16
F32 = jnp.float32
VECTORS = 5


def own_row(flip, rows, row):
    return flip * (rows - 1) + (1 - 2 * flip) * row


def run_copies(copies, sems):
    copies = [pltpu.make_async_copy(a, b, sems.at[i]) for i, (a, b) in enumerate(copies)]
    for copy in copies:
        copy.start()
    return copies


def rows_kernel(flags, images, *rest):
    micros, rows = images.shape[:2]
    sems = rest[-1]
    copies = []
    for m in range(micros):
        near, far, cross = rest[2 * m], rest[2 * m + 1], rest[2 * micros]
        for row in range(rows):
            here = images.at[m, own_row(flags[1], rows, row)]
            if m == micros - 1:
                copies.append((here, far.at[row]))
                if row < NEAR:
                    copies.append((here, near.at[row]))
            else:
                copies.append((here, near.at[row] if row < NEAR else far.at[row - NEAR]))
            if row >= rows - CROSS:
                copies.append((here, cross.at[m, row - (rows - CROSS)]))
    for copy in run_copies(copies, sems):
        copy.wait()


def mirrored_rows(flags, images):
    micros, rows, width, channels = images.shape
    counts = [NEAR, rows - NEAR] * (micros - 1) + [NEAR, rows]
    return pl.pallas_call(
        rows_kernel,
        out_shape=[pltpu.VMEM((count, width, channels), BF) for count in counts]
        + [pltpu.VMEM((micros, CROSS, width, channels), BF)],
        in_specs=[pl.BlockSpec(memory_space=pltpu.SMEM), pl.BlockSpec(memory_space=pltpu.HBM)],
        out_specs=[pl.BlockSpec(memory_space=pltpu.VMEM)] * (2 * micros + 1),
        scratch_shapes=[pltpu.SemaphoreType.DMA((micros * (rows + CROSS) + NEAR,))],
        compiler_params=pltpu.CompilerParams(vmem_limit_bytes=2**20),
        cost_estimate=pl.CostEstimate(flops=0, bytes_accessed=2 * rows * width * channels, transcendentals=0),
        name="mirrored_rows",
    )(flags, pltpu.with_memory_space_constraint(images, pltpu.HBM))


def setup_kernel(flags, weight, conv_bias, gain, shift, b_out, scale, b_in, taps, vectors, inner, select, raw, sems):
    copies = [(v, vectors.at[i]) for i, v in enumerate((conv_bias, gain, shift, b_out, scale))]
    copies += [(b_in, inner)]
    copies += [(weight.at[0, jnp.where(flags[1] == 1, TAPS - 1 - i, i)], raw.at[i]) for i in range(TAPS)]
    copies = run_copies(copies, sems)
    width, depth = select.shape
    at = lax.broadcasted_iota(jnp.int32, (width, depth), 0)
    entry = lax.broadcasted_iota(jnp.int32, (width, depth), 1)
    hit = jnp.zeros((width, depth), jnp.bool_)
    for col in range(TAPS):
        hit = hit | ((entry - col * width == at + col - REACH) & (entry >= col * width) & (entry < (col + 1) * width))
    select[...] = hit.astype(F32).astype(BF)
    for copy in copies:
        copy.wait()
    for off in range(TAPS):
        rows = raw[off].astype(F32)
        for col in range(TAPS):
            one = jnp.broadcast_to(rows[col : col + 1, :], (SUBLANES, rows.shape[1]))
            taps[off * TAPS + col] = one.astype(BF)


def setup(flags, weight, vectors, b_in, width):
    channels = weight.shape[-1]
    operands = [pltpu.with_memory_space_constraint(v, pltpu.HBM) for v in (weight, *vectors, b_in)]
    return pl.pallas_call(
        setup_kernel,
        out_shape=[
            pltpu.VMEM((TAPS * TAPS, SUBLANES, channels), BF),
            pltpu.VMEM((VECTORS, 1, channels), F32),
            pltpu.VMEM(b_in.shape, F32),
            pltpu.VMEM((width, TAPS * width), BF),
        ],
        in_specs=[pl.BlockSpec(memory_space=pltpu.SMEM)] + [pl.BlockSpec(memory_space=pltpu.HBM)] * len(operands),
        out_specs=[pl.BlockSpec(memory_space=pltpu.VMEM)] * 4,
        scratch_shapes=[
            pltpu.VMEM((TAPS, TAPS, channels), BF),
            pltpu.SemaphoreType.DMA((VECTORS + 1 + TAPS,)),
        ],
        compiler_params=pltpu.CompilerParams(vmem_limit_bytes=4 * 2**20),
        cost_estimate=pl.CostEstimate(flops=0, bytes_accessed=2**22, transcendentals=0),
        name="setup",
    )(flags, *operands)


def block_kernel(micro, last, final, chunk, *refs):
    refs = list(refs)
    if last:
        whole = refs.pop(1)
        rows, width, channels = whole.shape
        near, far = whole.at[:NEAR], whole.at[NEAR:]
    else:
        near, far = refs.pop(1), refs.pop(1)
        rows, width, channels = near.shape[0] + far.shape[0], near.shape[1], near.shape[2]
    flags, swap, cross, taps, vectors, inner_bias, select, w_in_hbm, w_out_hbm = refs[:9]
    w_in, w_out, sums, normal, total, *tail = refs[-7 if last else -6 :]
    sems = tail[-1]
    outs = refs[9 : -7 if last else -6]
    if last:
        earlier, stash, result = outs[0], outs[-1], tail[0]
    else:
        result = outs[-1]
    near_out, far_out, cross_out = (None, None, None) if final else outs[-4:-1]
    if last and not final:
        whole_out = far_out
        far_out = whole_out.at[NEAR:]
    cross = cross.at[micro] if len(cross.shape) == 4 else cross
    hidden = w_in.shape[1]
    conv_bias, gain, shift, b_out, scale = (vectors.at[i] for i in range(VECTORS))

    def source(row, lanes):
        if row < REACH:
            return swap[REACH - 1 - row, :, lanes]
        if row < REACH + NEAR:
            return near[row - REACH, :, lanes]
        if row < REACH + rows:
            return far[row - REACH - NEAR, :, lanes]
        return cross[REACH + CROSS + rows - 1 - row, :, lanes]

    @pl.when(flags[0] == 1)
    def _():
        get_in = pltpu.make_async_copy(w_in_hbm, w_in, sems.at[0])
        get_out = pltpu.make_async_copy(w_out_hbm, w_out, sems.at[1])
        get_in.start()
        get_out.start()
        if last:
            keep_earlier = pltpu.make_async_copy(earlier, stash.at[0, micro - 1], sems.at[2])
            keep_earlier.start()
        @pl.loop(0, channels // LANES)
        def _(group):
            lanes = pl.ds(pl.multiple_of(group * LANES, LANES), LANES)
            inputs = [source(row, lanes) for row in range(rows + 2 * REACH)]
            for col in range(TAPS):
                parts = [None] * rows
                for off in range(TAPS):
                    tap = taps[off * TAPS + col, :, lanes]
                    tap = jnp.concatenate([tap] * (width // SUBLANES), axis=0)
                    for row in range(rows):
                        term = inputs[row + off] * tap
                        parts[row] = term if off == 0 else parts[row] + term
                for row in range(rows):
                    sums[row, col * width : (col + 1) * width, lanes] = parts[row]

        @pl.loop(0, rows, unroll=2)
        def _(row):
            conv = jnp.dot(select[...], sums[row], preferred_element_type=F32) + conv_bias[...]
            centred = conv - jnp.mean(conv, axis=-1, keepdims=True)
            var = jnp.mean(centred * centred, axis=-1, keepdims=True)
            normed = (centred * lax.rsqrt(var + 1e-06) * gain[...] + shift[...]).astype(BF)
            normal[pl.ds(pl.multiple_of(row * width, width), width), :] = normed

        get_in.wait()
        for start in range(0, hidden, chunk):
            part = slice(start, start + chunk)
            inner = jnp.dot(normal[...], w_in[:, part], preferred_element_type=F32) + inner_bias[:, part]
            act = (0.5 * inner * (1.0 + lax.erf(inner * np.float32(0.5**0.5)))).astype(BF)
            if start == 0:
                get_out.wait()
            branch = jnp.dot(act, w_out[part, :], preferred_element_type=F32)
            if start == 0:
                total[...] = branch
            else:
                total[...] += branch
        def outcome(row, value):
            branch = total[pl.ds(pl.multiple_of(row * width, width), width), :] + b_out[...]
            value = (value.astype(F32) + scale[...] * branch).astype(BF)
            result[own_row(flags[1], rows, row)] = value
            return value

        @pl.loop(0, NEAR)
        def _(row):
            value = outcome(row, near[row])
            if not final:
                near_out[row] = value
                if last:
                    whole_out[row] = value

        @pl.loop(0, rows - NEAR)
        def _(row):
            value = outcome(row + NEAR, far[row])
            if not final:
                far_out[row] = value
                if rows - NEAR == CROSS:
                    cross_out[row] = value
                else:

                    @pl.when(row >= rows - NEAR - CROSS)
                    def _():
                        cross_out[jnp.maximum(row - (rows - NEAR - CROSS), 0)] = value

        if last:
            keep = pltpu.make_async_copy(result, stash.at[0, micro], sems.at[3])
            keep.start()
            keep_earlier.wait()
            keep.wait()


def run_block(micro, micros, final, flags, halo, params, weights, earlier, stash):
    last = micro == micros - 1
    own = halo[:1] if last else halo[:2]
    rows, (width, channels) = sum(v.shape[0] for v in own), own[0].shape[1:]
    vmem = pl.BlockSpec(memory_space=pltpu.VMEM)
    anywhere = pl.BlockSpec(memory_space=pl.ANY)
    held = [pltpu.with_memory_space_constraint(v, pltpu.VMEM) for v in [*halo, *params]]
    pinned = [pltpu.with_memory_space_constraint(v, pltpu.HBM) for v in weights]
    operands = [flags] + held + pinned
    specs = [pl.BlockSpec(memory_space=pltpu.SMEM)] + [vmem] * len(held)
    specs += [pl.BlockSpec(memory_space=pltpu.HBM)] * len(pinned)
    counts = () if final else (NEAR, rows if last else rows - NEAR, CROSS)
    out_shape = [pltpu.VMEM((count, width, channels), BF) for count in counts]
    scratch = [
        pltpu.VMEM(weights[0].shape, BF),
        pltpu.VMEM(weights[1].shape, BF),
        pltpu.VMEM((rows, TAPS * width, channels), BF),
        pltpu.VMEM((rows * width, channels), BF),
        pltpu.VMEM((rows * width, channels), F32),
    ]
    result = pltpu.VMEM((rows, width, channels), BF)
    out_specs = [vmem] * len(out_shape)
    aliases = {}
    if last:
        operands.append(pltpu.with_memory_space_constraint(earlier, pltpu.VMEM))
        specs.append(vmem)
        if stash is not None:
            aliases = {len(operands): len(out_shape)}
            operands.append(stash)
            specs.append(anywhere)
        out_shape.append(jax.ShapeDtypeStruct((1, micros, rows, width, channels), BF))
        out_specs.append(anywhere)
        scratch.append(result)
    else:
        out_shape.append(result)
        out_specs.append(vmem)
    *relayed, kept = pl.pallas_call(
        functools.partial(block_kernel, micro, last, final, 768),
        out_shape=out_shape,
        in_specs=specs,
        out_specs=out_specs,
        scratch_shapes=scratch + [pltpu.SemaphoreType.DMA((4,))],
        input_output_aliases=aliases,
        compiler_params=pltpu.CompilerParams(vmem_limit_bytes=32 * 2**20),
        cost_estimate=pl.CostEstimate(flops=2**20 if last else 2**33, bytes_accessed=2**10, transcendentals=0),
        name="block",
    )(*operands)
    return relayed, kept


def body(images, dw_weight, dw_bias, ln_gain, ln_bias, w_in, b_in, w_out, b_out, layer_scale):
    segment = lax.axis_index("segment")
    sections = lax.axis_size("segment")
    place = lax.axis_index("dp")
    places = lax.axis_size("dp")
    micros, rows, width, channels = images.shape
    per_image = SIDE // rows
    half = per_image // 2
    reverse = (place % 2 == 0).astype(jnp.int32)
    flags = [jnp.stack([(segment == section).astype(jnp.int32), reverse]) for section in range(sections)]

    axes = ("segment", "dp")

    def index(section, p):
        return section % sections * places + p % places

    facing = {}
    for p in range(places):
        if (p + half) % per_image in (half - 1, half):
            facing[p] = p + 1 if p % 2 == 1 else p - 1
    swap_pairs = [(index(s, p), index(s, p ^ 1)) for s in range(sections) for p in range(places)]
    near_pairs = [(index(s, p), index(s, q)) for s in range(sections) for p, q in facing.items()]

    def relay_pairs(section, onward):
        return [(index(section, p), index(section + 1, q)) for p, q in onward.items()]

    same = {p: p for p in range(places)}
    other = {p: p ^ 1 for p in range(places)}

    *parts, cross = mirrored_rows(flags[0], images)
    cross = lax.ppermute(cross, axes, near_pairs)
    params = setup(flags[0], dw_weight, (dw_bias, ln_gain, ln_bias, b_out, layer_scale), b_in, width)
    weights = (w_in[0], w_out[0])

    halos = []
    for m in range(micros):
        near, far = parts[2 * m : 2 * m + 2]
        if m == micros - 1:
            halos.append((far, lax.ppermute(near, axes, swap_pairs), cross))
        else:
            halos.append((near, far, None, cross))
    stash = before = None
    for section in range(sections):
        later, earlier = [], None
        for m in range(micros):
            halo = halos[m]
            if m < micros - 1:
                near, far, _, cross = halo
                if section > 0:
                    near, _ = lax.optimization_barrier((near, before))
                halo = (near, far, lax.ppermute(near, axes, swap_pairs), cross)
            final = section == sections - 1
            relayed, kept = run_block(m, micros, final, flags[section], halo, params, weights, earlier, stash)
            before = kept
            if m == micros - 1:
                stash = kept
            else:
                earlier = kept
            if not final:
                if m < micros - 1:
                    near = lax.ppermute(relayed[0], axes, relay_pairs(section, same))
                    cross = lax.ppermute(relayed[2], axes, relay_pairs(section, facing))
                    far = lax.ppermute(relayed[1], axes, relay_pairs(section, same))
                    later.append((near, far, None, cross))
                else:
                    near = lax.ppermute(relayed[0], axes, relay_pairs(section, other))
                    cross = lax.ppermute(relayed[2], axes, relay_pairs(section, facing))
                    whole = lax.ppermute(relayed[1], axes, relay_pairs(section, same))
                    later.append((whole, near, cross))
        halos = later
    return stash


def solution(mesh):
    in_specs = (
        P(None, "dp", None, None),
        P("segment", None, None, None),
        P("segment", None),
        P("segment", None),
        P("segment", None),
        P("segment", None, None),
        P("segment", None),
        P("segment", None, None),
        P("segment", None),
        P("segment", None),
    )
    out_specs = P("segment", None, "dp", None, None)
    return jax.shard_map(body, mesh=mesh, in_specs=in_specs, out_specs=out_specs, check_vma=False)
```

```python
import functools

import jax
import jax.numpy as jnp
import numpy as np
from jax import lax
from jax.experimental import pallas as pl
from jax.experimental.pallas import tpu as pltpu
from jax.sharding import PartitionSpec as P

SIDE = 32
TAPS = 7
REACH = 3
CROSS = 3
NEAR = 3
LANES = 128
SUBLANES = 16
BF = jnp.bfloat16
F32 = jnp.float32
VECTORS = 5


def own_row(flip, rows, row):
    return flip * (rows - 1) + (1 - 2 * flip) * row


def run_copies(copies, sems):
    copies = [pltpu.make_async_copy(a, b, sems.at[i]) for i, (a, b) in enumerate(copies)]
    for copy in copies:
        copy.start()
    return copies


def rows_kernel(flags, images, *rest):
    micros, rows = images.shape[:2]
    sems = rest[-1]
    copies = []
    for m in range(micros):
        near, far, cross = rest[m], rest[micros + m], rest[2 * micros]
        for row in range(rows):
            here = images.at[m, own_row(flags[1], rows, row)]
            copies.append((here, near.at[row] if row < NEAR else far.at[row - NEAR]))
            if row >= rows - CROSS:
                copies.append((here, cross.at[m, row - (rows - CROSS)]))
    for copy in run_copies(copies, sems):
        copy.wait()


def mirrored_rows(flags, images):
    micros, rows, width, channels = images.shape
    return pl.pallas_call(
        rows_kernel,
        out_shape=[pltpu.VMEM((NEAR, width, channels), BF)] * micros
        + [pltpu.VMEM((rows - NEAR, width, channels), BF)] * micros
        + [pltpu.VMEM((micros, CROSS, width, channels), BF)],
        in_specs=[pl.BlockSpec(memory_space=pltpu.SMEM), pl.BlockSpec(memory_space=pltpu.HBM)],
        out_specs=[pl.BlockSpec(memory_space=pltpu.VMEM)] * (2 * micros + 1),
        scratch_shapes=[pltpu.SemaphoreType.DMA((micros * (rows + CROSS),))],
        compiler_params=pltpu.CompilerParams(vmem_limit_bytes=2**20),
        cost_estimate=pl.CostEstimate(flops=0, bytes_accessed=2 * rows * width * channels, transcendentals=0),
        name="mirrored_rows",
    )(flags, pltpu.with_memory_space_constraint(images, pltpu.HBM))


def setup_kernel(flags, weight, conv_bias, gain, shift, b_out, scale, b_in, taps, vectors, inner, select, raw, sems):
    copies = [(v, vectors.at[i]) for i, v in enumerate((conv_bias, gain, shift, b_out, scale))]
    copies += [(b_in, inner)]
    copies += [(weight.at[0, jnp.where(flags[1] == 1, TAPS - 1 - i, i)], raw.at[i]) for i in range(TAPS)]
    copies = run_copies(copies, sems)
    width, depth = select.shape
    at = lax.broadcasted_iota(jnp.int32, (width, depth), 0)
    entry = lax.broadcasted_iota(jnp.int32, (width, depth), 1)
    hit = jnp.zeros((width, depth), jnp.bool_)
    for col in range(TAPS):
        hit = hit | ((entry - col * width == at + col - REACH) & (entry >= col * width) & (entry < (col + 1) * width))
    select[...] = hit.astype(F32).astype(BF)
    for copy in copies:
        copy.wait()
    for off in range(TAPS):
        rows = raw[off].astype(F32)
        for col in range(TAPS):
            one = jnp.broadcast_to(rows[col : col + 1, :], (SUBLANES, rows.shape[1]))
            taps[off * TAPS + col] = one.astype(BF)


def setup(flags, weight, vectors, b_in, width):
    channels = weight.shape[-1]
    operands = [pltpu.with_memory_space_constraint(v, pltpu.HBM) for v in (weight, *vectors, b_in)]
    return pl.pallas_call(
        setup_kernel,
        out_shape=[
            pltpu.VMEM((TAPS * TAPS, SUBLANES, channels), BF),
            pltpu.VMEM((VECTORS, 1, channels), F32),
            pltpu.VMEM(b_in.shape, F32),
            pltpu.VMEM((width, TAPS * width), BF),
        ],
        in_specs=[pl.BlockSpec(memory_space=pltpu.SMEM)] + [pl.BlockSpec(memory_space=pltpu.HBM)] * len(operands),
        out_specs=[pl.BlockSpec(memory_space=pltpu.VMEM)] * 4,
        scratch_shapes=[
            pltpu.VMEM((TAPS, TAPS, channels), BF),
            pltpu.SemaphoreType.DMA((VECTORS + 1 + TAPS,)),
        ],
        compiler_params=pltpu.CompilerParams(vmem_limit_bytes=4 * 2**20),
        cost_estimate=pl.CostEstimate(flops=0, bytes_accessed=2**22, transcendentals=0),
        name="setup",
    )(flags, *operands)


def block_kernel(micro, last, final, chunk, *refs):
    refs = list(refs)
    flags, near, far, swap, cross, taps, vectors, inner_bias, select, w_in_hbm, w_out_hbm = refs[:11]
    w_in, w_out, sums, normal, total, *tail = refs[-7 if last else -6 :]
    sems = tail[-1]
    outs = refs[11 : -7 if last else -6]
    if last:
        earlier, stash, result = outs[0], outs[-1], tail[0]
    else:
        result = outs[-1]
    near_out, far_out, cross_out = (None, None, None) if final else outs[-4:-1]
    rows, width, channels = near.shape[0] + far.shape[0], near.shape[1], near.shape[2]
    cross = cross.at[micro] if len(cross.shape) == 4 else cross
    hidden = w_in.shape[1]
    conv_bias, gain, shift, b_out, scale = (vectors.at[i] for i in range(VECTORS))

    def source(row, lanes):
        if row < REACH:
            return swap[REACH - 1 - row, :, lanes]
        if row < REACH + NEAR:
            return near[row - REACH, :, lanes]
        if row < REACH + rows:
            return far[row - REACH - NEAR, :, lanes]
        return cross[REACH + CROSS + rows - 1 - row, :, lanes]

    @pl.when(flags[0] == 1)
    def _():
        get_in = pltpu.make_async_copy(w_in_hbm, w_in, sems.at[0])
        get_out = pltpu.make_async_copy(w_out_hbm, w_out, sems.at[1])
        get_in.start()
        get_out.start()
        if last:
            keep_earlier = pltpu.make_async_copy(earlier, stash.at[0, micro - 1], sems.at[2])
            keep_earlier.start()
        @pl.loop(0, channels // LANES)
        def _(group):
            lanes = pl.ds(pl.multiple_of(group * LANES, LANES), LANES)
            inputs = [source(row, lanes) for row in range(rows + 2 * REACH)]
            for col in range(TAPS):
                parts = [None] * rows
                for off in range(TAPS):
                    tap = taps[off * TAPS + col, :, lanes]
                    tap = jnp.concatenate([tap] * (width // SUBLANES), axis=0)
                    for row in range(rows):
                        term = inputs[row + off] * tap
                        parts[row] = term if off == 0 else parts[row] + term
                for row in range(rows):
                    sums[row, col * width : (col + 1) * width, lanes] = parts[row]

        @pl.loop(0, rows, unroll=8)
        def _(row):
            conv = jnp.dot(select[...], sums[row], preferred_element_type=F32) + conv_bias[...]
            centred = conv - jnp.mean(conv, axis=-1, keepdims=True)
            var = jnp.mean(centred * centred, axis=-1, keepdims=True)
            normed = (centred * lax.rsqrt(var + 1e-06) * gain[...] + shift[...]).astype(BF)
            normal[pl.ds(pl.multiple_of(row * width, width), width), :] = normed

        get_in.wait()
        for start in range(0, hidden, chunk):
            part = slice(start, start + chunk)
            inner = jnp.dot(normal[...], w_in[:, part], preferred_element_type=F32) + inner_bias[:, part]
            act = (0.5 * inner * (1.0 + lax.erf(inner * np.float32(0.5**0.5)))).astype(BF)
            if start == 0:
                get_out.wait()
            branch = jnp.dot(act, w_out[part, :], preferred_element_type=F32)
            if start == 0:
                total[...] = branch
            else:
                total[...] += branch
        def outcome(row, value):
            branch = total[pl.ds(pl.multiple_of(row * width, width), width), :] + b_out[...]
            value = (value.astype(F32) + scale[...] * branch).astype(BF)
            result[own_row(flags[1], rows, row)] = value
            if last:
                keep(row).start()
            return value

        def keep(row):
            at = own_row(flags[1], rows, row)
            return pltpu.make_async_copy(result.at[at], stash.at[0, micro, at], sems.at[3])

        @pl.loop(0, NEAR, unroll=True)
        def _(row):
            value = outcome(row, near[row])
            if not final:
                near_out[row] = value

        @pl.loop(0, rows - NEAR, unroll=True)
        def _(row):
            value = outcome(row + NEAR, far[row])
            if not final:
                far_out[row] = value
                if rows - NEAR == CROSS:
                    cross_out[row] = value
                else:

                    @pl.when(row >= rows - NEAR - CROSS)
                    def _():
                        cross_out[jnp.maximum(row - (rows - NEAR - CROSS), 0)] = value

        if last:
            keep_earlier.wait()
            pltpu.make_async_copy(result, stash.at[0, micro], sems.at[3]).wait()


def run_block(micro, micros, final, flags, halo, params, weights, earlier, stash):
    last = micro == micros - 1
    near, far = halo[:2]
    rows, width, channels = near.shape[0] + far.shape[0], near.shape[1], near.shape[2]
    vmem = pl.BlockSpec(memory_space=pltpu.VMEM)
    anywhere = pl.BlockSpec(memory_space=pl.ANY)
    held = [pltpu.with_memory_space_constraint(v, pltpu.VMEM) for v in [*halo, *params]]
    pinned = [pltpu.with_memory_space_constraint(v, pltpu.HBM) for v in weights]
    operands = [flags] + held + pinned
    specs = [pl.BlockSpec(memory_space=pltpu.SMEM)] + [vmem] * len(held)
    specs += [pl.BlockSpec(memory_space=pltpu.HBM)] * len(pinned)
    counts = () if final else (NEAR, rows - NEAR, CROSS)
    out_shape = [pltpu.VMEM((count, width, channels), BF) for count in counts]
    scratch = [
        pltpu.VMEM(weights[0].shape, BF),
        pltpu.VMEM(weights[1].shape, BF),
        pltpu.VMEM((rows, TAPS * width, channels), BF),
        pltpu.VMEM((rows * width, channels), BF),
        pltpu.VMEM((rows * width, channels), F32),
    ]
    result = pltpu.VMEM((rows, width, channels), BF)
    out_specs = [vmem] * len(out_shape)
    aliases = {}
    if last:
        operands.append(pltpu.with_memory_space_constraint(earlier, pltpu.VMEM))
        specs.append(vmem)
        if stash is not None:
            aliases = {len(operands): len(out_shape)}
            operands.append(stash)
            specs.append(anywhere)
        out_shape.append(jax.ShapeDtypeStruct((1, micros, rows, width, channels), BF))
        out_specs.append(anywhere)
        scratch.append(result)
    else:
        out_shape.append(result)
        out_specs.append(vmem)
    *relayed, kept = pl.pallas_call(
        functools.partial(block_kernel, micro, last, final, 768),
        out_shape=out_shape,
        in_specs=specs,
        out_specs=out_specs,
        scratch_shapes=scratch + [pltpu.SemaphoreType.DMA((4,))],
        input_output_aliases=aliases,
        compiler_params=pltpu.CompilerParams(vmem_limit_bytes=32 * 2**20),
        cost_estimate=pl.CostEstimate(flops=2**33 if last else 2**33, bytes_accessed=2**10, transcendentals=0),
        name="block",
    )(*operands)
    return relayed, kept


def body(images, dw_weight, dw_bias, ln_gain, ln_bias, w_in, b_in, w_out, b_out, layer_scale):
    segment = lax.axis_index("segment")
    sections = lax.axis_size("segment")
    place = lax.axis_index("dp")
    places = lax.axis_size("dp")
    micros, rows, width, channels = images.shape
    per_image = SIDE // rows
    half = per_image // 2
    reverse = (place % 2 == 0).astype(jnp.int32)
    flags = [jnp.stack([(segment == section).astype(jnp.int32), reverse]) for section in range(sections)]

    axes = ("segment", "dp")

    def index(section, p):
        return section % sections * places + p % places

    facing = {}
    for p in range(places):
        if (p + half) % per_image in (half - 1, half):
            facing[p] = p + 1 if p % 2 == 1 else p - 1
    swap_pairs = [(index(s, p), index(s, p ^ 1)) for s in range(sections) for p in range(places)]
    near_pairs = [(index(s, p), index(s, q)) for s in range(sections) for p, q in facing.items()]

    def relay_pairs(section, onward):
        return [(index(section, p), index(section + 1, q)) for p, q in onward.items()]

    same = {p: p for p in range(places)}

    *parts, cross = mirrored_rows(flags[0], images)
    cross = lax.ppermute(cross, axes, near_pairs)
    params = setup(flags[0], dw_weight, (dw_bias, ln_gain, ln_bias, b_out, layer_scale), b_in, width)
    weights = (w_in[0], w_out[0])

    halos = [(parts[m], parts[micros + m], cross) for m in range(micros)]
    stash = before = None
    for section in range(sections):
        later, earlier = [], None
        for m in range(micros):
            near, far, cross = halos[m]
            if section > 0:
                near, _ = lax.optimization_barrier((near, before))
            swap = lax.ppermute(near, axes, swap_pairs)
            halo = (near, far, swap, cross)
            final = section == sections - 1
            relayed, kept = run_block(m, micros, final, flags[section], halo, params, weights, earlier, stash)
            before = kept
            if m == micros - 1:
                stash = kept
            else:
                earlier = kept
            if not final:
                near = lax.ppermute(relayed[0], axes, relay_pairs(section, same))
                cross = lax.ppermute(relayed[2], axes, relay_pairs(section, facing))
                far = lax.ppermute(relayed[1], axes, relay_pairs(section, same))
                later.append((near, far, cross))
        halos = later
    return stash


def solution(mesh):
    in_specs = (
        P(None, "dp", None, None),
        P("segment", None, None, None),
        P("segment", None),
        P("segment", None),
        P("segment", None),
        P("segment", None, None),
        P("segment", None),
        P("segment", None, None),
        P("segment", None),
        P("segment", None),
    )
    out_specs = P("segment", None, "dp", None, None)
    return jax.shard_map(body, mesh=mesh, in_specs=in_specs, out_specs=out_specs, check_vma=False)
```

```python
import functools

import jax
import jax.numpy as jnp
import numpy as np
from jax import lax
from jax.experimental import pallas as pl
from jax.experimental.pallas import tpu as pltpu
from jax.sharding import PartitionSpec as P

SIDE = 32
TAPS = 7
REACH = 3
CROSS = 3
NEAR = 3
LANES = 128
SUBLANES = 16
BF = jnp.bfloat16
F32 = jnp.float32
VECTORS = 5


def own_row(flip, rows, row):
    return flip * (rows - 1) + (1 - 2 * flip) * row


def run_copies(copies, sems):
    copies = [pltpu.make_async_copy(a, b, sems.at[i]) for i, (a, b) in enumerate(copies)]
    for copy in copies:
        copy.start()
    return copies


def cross_kernel(flags, images, cross, sems):
    micros, rows = images.shape[:2]
    copies = []
    for m in range(micros):
        for row in range(rows - CROSS, rows):
            copies.append((images.at[m, own_row(flags[1], rows, row)], cross.at[m, row - (rows - CROSS)]))
    for copy in run_copies(copies, sems):
        copy.wait()


def rows_kernel(flags, images, *rest):
    micros, rows = images.shape[:2]
    sems = rest[-1]
    copies = []
    for m in range(micros):
        near, far = rest[m], rest[micros + m]
        for row in range(rows):
            here = images.at[m, own_row(flags[1], rows, row)]
            copies.append((here, near.at[row] if row < NEAR else far.at[row - NEAR]))
    for copy in run_copies(copies, sems):
        copy.wait()


def mirrored_rows(kernel, name, flags, images, shapes, copies):
    return pl.pallas_call(
        kernel,
        out_shape=[pltpu.VMEM(shape, BF) for shape in shapes],
        in_specs=[pl.BlockSpec(memory_space=pltpu.SMEM), pl.BlockSpec(memory_space=pltpu.HBM)],
        out_specs=[pl.BlockSpec(memory_space=pltpu.VMEM)] * len(shapes),
        scratch_shapes=[pltpu.SemaphoreType.DMA((copies,))],
        compiler_params=pltpu.CompilerParams(vmem_limit_bytes=2**20),
        cost_estimate=pl.CostEstimate(flops=0, bytes_accessed=2**21, transcendentals=0),
        name=name,
    )(flags, pltpu.with_memory_space_constraint(images, pltpu.HBM))


def setup_kernel(flags, weight, conv_bias, gain, shift, b_out, scale, b_in, taps, vectors, inner, select, raw, sems):
    copies = [(v, vectors.at[i]) for i, v in enumerate((conv_bias, gain, shift, b_out, scale))]
    copies += [(b_in, inner)]
    copies += [(weight.at[0, jnp.where(flags[1] == 1, TAPS - 1 - i, i)], raw.at[i]) for i in range(TAPS)]
    copies = run_copies(copies, sems)
    width, depth = select.shape
    at = lax.broadcasted_iota(jnp.int32, (width, depth), 0)
    entry = lax.broadcasted_iota(jnp.int32, (width, depth), 1)
    hit = jnp.zeros((width, depth), jnp.bool_)
    for col in range(TAPS):
        hit = hit | ((entry - col * width == at + col - REACH) & (entry >= col * width) & (entry < (col + 1) * width))
    select[...] = hit.astype(F32).astype(BF)
    for copy in copies:
        copy.wait()
    for off in range(TAPS):
        rows = raw[off].astype(F32)
        for col in range(TAPS):
            one = jnp.broadcast_to(rows[col : col + 1, :], (SUBLANES, rows.shape[1]))
            taps[off * TAPS + col] = one.astype(BF)


def setup(flags, weight, vectors, b_in, width):
    channels = weight.shape[-1]
    operands = [pltpu.with_memory_space_constraint(v, pltpu.HBM) for v in (weight, *vectors, b_in)]
    return pl.pallas_call(
        setup_kernel,
        out_shape=[
            pltpu.VMEM((TAPS * TAPS, SUBLANES, channels), BF),
            pltpu.VMEM((VECTORS, 1, channels), F32),
            pltpu.VMEM(b_in.shape, F32),
            pltpu.VMEM((width, TAPS * width), BF),
        ],
        in_specs=[pl.BlockSpec(memory_space=pltpu.SMEM)] + [pl.BlockSpec(memory_space=pltpu.HBM)] * len(operands),
        out_specs=[pl.BlockSpec(memory_space=pltpu.VMEM)] * 4,
        scratch_shapes=[
            pltpu.VMEM((TAPS, TAPS, channels), BF),
            pltpu.SemaphoreType.DMA((VECTORS + 1 + TAPS,)),
        ],
        compiler_params=pltpu.CompilerParams(vmem_limit_bytes=4 * 2**20),
        cost_estimate=pl.CostEstimate(flops=0, bytes_accessed=2**22, transcendentals=0),
        name="setup",
    )(flags, *operands)


def block_kernel(micro, last, final, chunk, *refs):
    refs = list(refs)
    flags, near, far, swap, cross, taps, vectors, inner_bias, select, w_in_hbm, w_out_hbm = refs[:11]
    w_in, w_out, sums, normal, total, *tail = refs[-7 if last else -6 :]
    sems = tail[-1]
    outs = refs[11 : -7 if last else -6]
    if last:
        earlier, stash, result = outs[0], outs[-1], tail[0]
    else:
        result = outs[-1]
    near_out, far_out, cross_out = (None, None, None) if final else outs[-4:-1]
    rows, width, channels = near.shape[0] + far.shape[0], near.shape[1], near.shape[2]
    cross = cross.at[micro] if len(cross.shape) == 4 else cross
    hidden = w_in.shape[1]
    conv_bias, gain, shift, b_out, scale = (vectors.at[i] for i in range(VECTORS))

    def source(row, lanes):
        if row < REACH:
            return swap[REACH - 1 - row, :, lanes]
        if row < REACH + NEAR:
            return near[row - REACH, :, lanes]
        if row < REACH + rows:
            return far[row - REACH - NEAR, :, lanes]
        return cross[REACH + CROSS + rows - 1 - row, :, lanes]

    @pl.when(flags[0] == 1)
    def _():
        get_in = pltpu.make_async_copy(w_in_hbm, w_in, sems.at[0])
        get_out = pltpu.make_async_copy(w_out_hbm, w_out, sems.at[1])
        get_in.start()
        get_out.start()
        if last:
            keep_earlier = pltpu.make_async_copy(earlier, stash.at[0, micro - 1], sems.at[2])
            keep_earlier.start()
        @pl.loop(0, channels // LANES)
        def _(group):
            lanes = pl.ds(pl.multiple_of(group * LANES, LANES), LANES)
            inputs = [source(row, lanes) for row in range(rows + 2 * REACH)]
            for col in range(TAPS):
                parts = [None] * rows
                for off in range(TAPS):
                    tap = taps[off * TAPS + col, :, lanes]
                    tap = jnp.concatenate([tap] * (width // SUBLANES), axis=0)
                    for row in range(rows):
                        term = inputs[row + off] * tap
                        parts[row] = term if off == 0 else parts[row] + term
                for row in range(rows):
                    sums[row, col * width : (col + 1) * width, lanes] = parts[row]

        @pl.loop(0, rows, unroll=8)
        def _(row):
            conv = jnp.dot(select[...], sums[row], preferred_element_type=F32) + conv_bias[...]
            centred = conv - jnp.mean(conv, axis=-1, keepdims=True)
            var = jnp.mean(centred * centred, axis=-1, keepdims=True)
            normed = (centred * lax.rsqrt(var + 1e-06) * gain[...] + shift[...]).astype(BF)
            normal[pl.ds(pl.multiple_of(row * width, width), width), :] = normed

        get_in.wait()
        for start in range(0, hidden, chunk):
            part = slice(start, start + chunk)
            inner = jnp.dot(normal[...], w_in[:, part], preferred_element_type=F32) + inner_bias[:, part]
            act = (0.5 * inner * (1.0 + lax.erf(inner * np.float32(0.5**0.5)))).astype(BF)
            if start == 0:
                get_out.wait()
            branch = jnp.dot(act, w_out[part, :], preferred_element_type=F32)
            if start == 0:
                total[...] = branch
            else:
                total[...] += branch
        def outcome(row, value):
            branch = total[pl.ds(pl.multiple_of(row * width, width), width), :] + b_out[...]
            value = (value.astype(F32) + scale[...] * branch).astype(BF)
            result[own_row(flags[1], rows, row)] = value
            if last:
                keep(row).start()
            return value

        def keep(row):
            at = own_row(flags[1], rows, row)
            return pltpu.make_async_copy(result.at[at], stash.at[0, micro, at], sems.at[3])

        @pl.loop(0, NEAR, unroll=True)
        def _(row):
            value = outcome(row, near[row])
            if not final:
                near_out[row] = value

        @pl.loop(0, rows - NEAR, unroll=True)
        def _(row):
            value = outcome(row + NEAR, far[row])
            if not final:
                far_out[row] = value
                if rows - NEAR == CROSS:
                    cross_out[row] = value
                else:

                    @pl.when(row >= rows - NEAR - CROSS)
                    def _():
                        cross_out[jnp.maximum(row - (rows - NEAR - CROSS), 0)] = value

        if last:
            keep_earlier.wait()
            pltpu.make_async_copy(result, stash.at[0, micro], sems.at[3]).wait()


def run_block(micro, micros, final, flags, halo, params, weights, earlier, stash):
    last = micro == micros - 1
    near, far = halo[:2]
    rows, width, channels = near.shape[0] + far.shape[0], near.shape[1], near.shape[2]
    vmem = pl.BlockSpec(memory_space=pltpu.VMEM)
    anywhere = pl.BlockSpec(memory_space=pl.ANY)
    held = [pltpu.with_memory_space_constraint(v, pltpu.VMEM) for v in [*halo, *params]]
    pinned = [pltpu.with_memory_space_constraint(v, pltpu.HBM) for v in weights]
    operands = [flags] + held + pinned
    specs = [pl.BlockSpec(memory_space=pltpu.SMEM)] + [vmem] * len(held)
    specs += [pl.BlockSpec(memory_space=pltpu.HBM)] * len(pinned)
    counts = () if final else (NEAR, rows - NEAR, CROSS)
    out_shape = [pltpu.VMEM((count, width, channels), BF) for count in counts]
    scratch = [
        pltpu.VMEM(weights[0].shape, BF),
        pltpu.VMEM(weights[1].shape, BF),
        pltpu.VMEM((rows, TAPS * width, channels), BF),
        pltpu.VMEM((rows * width, channels), BF),
        pltpu.VMEM((rows * width, channels), F32),
    ]
    result = pltpu.VMEM((rows, width, channels), BF)
    out_specs = [vmem] * len(out_shape)
    aliases = {}
    if last:
        operands.append(pltpu.with_memory_space_constraint(earlier, pltpu.VMEM))
        specs.append(vmem)
        if stash is not None:
            aliases = {len(operands): len(out_shape)}
            operands.append(stash)
            specs.append(anywhere)
        out_shape.append(jax.ShapeDtypeStruct((1, micros, rows, width, channels), BF))
        out_specs.append(anywhere)
        scratch.append(result)
    else:
        out_shape.append(result)
        out_specs.append(vmem)
    *relayed, kept = pl.pallas_call(
        functools.partial(block_kernel, micro, last, final, 768),
        out_shape=out_shape,
        in_specs=specs,
        out_specs=out_specs,
        scratch_shapes=scratch + [pltpu.SemaphoreType.DMA((4,))],
        input_output_aliases=aliases,
        compiler_params=pltpu.CompilerParams(vmem_limit_bytes=32 * 2**20),
        cost_estimate=pl.CostEstimate(flops=2**33 if last else 2**33, bytes_accessed=2**10, transcendentals=0),
        name="block",
    )(*operands)
    return relayed, kept


def body(images, dw_weight, dw_bias, ln_gain, ln_bias, w_in, b_in, w_out, b_out, layer_scale):
    segment = lax.axis_index("segment")
    sections = lax.axis_size("segment")
    place = lax.axis_index("dp")
    places = lax.axis_size("dp")
    micros, rows, width, channels = images.shape
    per_image = SIDE // rows
    half = per_image // 2
    reverse = (place % 2 == 0).astype(jnp.int32)
    flags = [jnp.stack([(segment == section).astype(jnp.int32), reverse]) for section in range(sections)]

    axes = ("segment", "dp")

    def index(section, p):
        return section % sections * places + p % places

    facing = {}
    for p in range(places):
        if (p + half) % per_image in (half - 1, half):
            facing[p] = p + 1 if p % 2 == 1 else p - 1
    swap_pairs = [(index(s, p), index(s, p ^ 1)) for s in range(sections) for p in range(places)]
    near_pairs = [(index(s, p), index(s, q)) for s in range(sections) for p, q in facing.items()]

    def relay_pairs(section, onward):
        return [(index(section, p), index(section + 1, q)) for p, q in onward.items()]

    same = {p: p for p in range(places)}

    shape = (micros, CROSS, width, channels)
    cross = mirrored_rows(cross_kernel, "cross_rows", flags[0], images, [shape], micros * CROSS)[0]
    cross = lax.ppermute(cross, axes, near_pairs)
    shapes = [(NEAR, width, channels)] * micros + [(rows - NEAR, width, channels)] * micros
    parts = mirrored_rows(rows_kernel, "own_rows", flags[0], images, shapes, micros * rows)
    params = setup(flags[0], dw_weight, (dw_bias, ln_gain, ln_bias, b_out, layer_scale), b_in, width)
    weights = (w_in[0], w_out[0])

    halos = [(parts[m], parts[micros + m], cross) for m in range(micros)]
    stash = before = None
    for section in range(sections):
        later, earlier = [], None
        for m in range(micros):
            near, far, cross = halos[m]
            if section > 0:
                near, _ = lax.optimization_barrier((near, before))
            swap = lax.ppermute(near, axes, swap_pairs)
            halo = (near, far, swap, cross)
            final = section == sections - 1
            relayed, kept = run_block(m, micros, final, flags[section], halo, params, weights, earlier, stash)
            before = kept
            if m == micros - 1:
                stash = kept
            else:
                earlier = kept
            if not final:
                near = lax.ppermute(relayed[0], axes, relay_pairs(section, same))
                cross = lax.ppermute(relayed[2], axes, relay_pairs(section, facing))
                far = lax.ppermute(relayed[1], axes, relay_pairs(section, same))
                later.append((near, far, cross))
        halos = later
    return stash


def solution(mesh):
    in_specs = (
        P(None, "dp", None, None),
        P("segment", None, None, None),
        P("segment", None),
        P("segment", None),
        P("segment", None),
        P("segment", None, None),
        P("segment", None),
        P("segment", None, None),
        P("segment", None),
        P("segment", None),
    )
    out_specs = P("segment", None, "dp", None, None)
    return jax.shard_map(body, mesh=mesh, in_specs=in_specs, out_specs=out_specs, check_vma=False)
```

```python
import functools

import jax
import jax.numpy as jnp
import numpy as np
from jax import lax
from jax.experimental import pallas as pl
from jax.experimental.pallas import tpu as pltpu
from jax.sharding import PartitionSpec as P

SIDE = 32
TAPS = 7
REACH = 3
CROSS = 3
NEAR = 3
LANES = 128
SUBLANES = 16
BF = jnp.bfloat16
F32 = jnp.float32
VECTORS = 5


def own_row(flip, rows, row):
    return flip * (rows - 1) + (1 - 2 * flip) * row


def run_copies(copies, sems):
    copies = [pltpu.make_async_copy(a, b, sems.at[i]) for i, (a, b) in enumerate(copies)]
    for copy in copies:
        copy.start()
    return copies


def cross_kernel(flags, images, cross, sems):
    micros, rows = images.shape[:2]
    copies = []
    for m in range(micros):
        for row in range(rows - CROSS, rows):
            copies.append((images.at[m, own_row(flags[1], rows, row)], cross.at[m, row - (rows - CROSS)]))
    for copy in run_copies(copies, sems):
        copy.wait()


def rows_kernel(flags, images, *rest):
    micros, rows = images.shape[:2]
    sems = rest[-1]
    copies = []
    for m in range(micros):
        near, far = rest[m], rest[micros + m]
        for row in range(rows):
            here = images.at[m, own_row(flags[1], rows, row)]
            copies.append((here, near.at[row] if row < NEAR else far.at[row - NEAR]))
    for copy in run_copies(copies, sems):
        copy.wait()


def mirrored_rows(kernel, name, flags, images, shapes, copies):
    return pl.pallas_call(
        kernel,
        out_shape=[pltpu.VMEM(shape, BF) for shape in shapes],
        in_specs=[pl.BlockSpec(memory_space=pltpu.SMEM), pl.BlockSpec(memory_space=pltpu.HBM)],
        out_specs=[pl.BlockSpec(memory_space=pltpu.VMEM)] * len(shapes),
        scratch_shapes=[pltpu.SemaphoreType.DMA((copies,))],
        compiler_params=pltpu.CompilerParams(vmem_limit_bytes=2**20),
        cost_estimate=pl.CostEstimate(flops=0, bytes_accessed=2**21, transcendentals=0),
        name=name,
    )(flags, pltpu.with_memory_space_constraint(images, pltpu.HBM))


def setup_kernel(flags, weight, conv_bias, gain, shift, b_out, scale, b_in, taps, vectors, inner, select, raw, sems):
    copies = [(v, vectors.at[i]) for i, v in enumerate((conv_bias, gain, shift, b_out, scale))]
    copies += [(b_in, inner)]
    copies += [(weight.at[0, jnp.where(flags[1] == 1, TAPS - 1 - i, i)], raw.at[i]) for i in range(TAPS)]
    copies = run_copies(copies, sems)
    width, depth = select.shape
    at = lax.broadcasted_iota(jnp.int32, (width, depth), 0)
    entry = lax.broadcasted_iota(jnp.int32, (width, depth), 1)
    hit = jnp.zeros((width, depth), jnp.bool_)
    for col in range(TAPS):
        hit = hit | ((entry - col * width == at + col - REACH) & (entry >= col * width) & (entry < (col + 1) * width))
    select[...] = hit.astype(F32).astype(BF)
    for copy in copies:
        copy.wait()
    for off in range(TAPS):
        rows = raw[off].astype(F32)
        for col in range(TAPS):
            one = jnp.broadcast_to(rows[col : col + 1, :], (SUBLANES, rows.shape[1]))
            taps[off * TAPS + col] = one.astype(BF)


def setup(flags, weight, vectors, b_in, width):
    channels = weight.shape[-1]
    operands = [pltpu.with_memory_space_constraint(v, pltpu.HBM) for v in (weight, *vectors, b_in)]
    return pl.pallas_call(
        setup_kernel,
        out_shape=[
            pltpu.VMEM((TAPS * TAPS, SUBLANES, channels), BF),
            pltpu.VMEM((VECTORS, 1, channels), F32),
            pltpu.VMEM(b_in.shape, F32),
            pltpu.VMEM((width, TAPS * width), BF),
        ],
        in_specs=[pl.BlockSpec(memory_space=pltpu.SMEM)] + [pl.BlockSpec(memory_space=pltpu.HBM)] * len(operands),
        out_specs=[pl.BlockSpec(memory_space=pltpu.VMEM)] * 4,
        scratch_shapes=[
            pltpu.VMEM((TAPS, TAPS, channels), BF),
            pltpu.SemaphoreType.DMA((VECTORS + 1 + TAPS,)),
        ],
        compiler_params=pltpu.CompilerParams(vmem_limit_bytes=4 * 2**20),
        cost_estimate=pl.CostEstimate(flops=0, bytes_accessed=2**22, transcendentals=0),
        name="setup",
    )(flags, *operands)


def block_kernel(micro, last, final, chunk, *refs):
    refs = list(refs)
    flags, near, far, swap, cross, taps, vectors, inner_bias, select, w_in_hbm, w_out_hbm = refs[:11]
    w_in, w_out, sums, normal, total, *tail = refs[-7 if last else -6 :]
    sems = tail[-1]
    outs = refs[11 : -7 if last else -6]
    if last:
        earlier, stash, result = outs[0], outs[-1], tail[0]
    else:
        result = outs[-1]
    near_out, far_out, cross_out = (None, None, None) if final else outs[-4:-1]
    rows, width, channels = near.shape[0] + far.shape[0], near.shape[1], near.shape[2]
    cross = cross.at[micro] if len(cross.shape) == 4 else cross
    hidden = w_in.shape[1]
    conv_bias, gain, shift, b_out, scale = (vectors.at[i] for i in range(VECTORS))

    def source(row, lanes):
        if row < REACH:
            return swap[REACH - 1 - row, :, lanes]
        if row < REACH + NEAR:
            return near[row - REACH, :, lanes]
        if row < REACH + rows:
            return far[row - REACH - NEAR, :, lanes]
        return cross[REACH + CROSS + rows - 1 - row, :, lanes]

    @pl.when(flags[0] == 1)
    def _():
        get_in = pltpu.make_async_copy(w_in_hbm, w_in, sems.at[0])
        get_out = pltpu.make_async_copy(w_out_hbm, w_out, sems.at[1])
        get_in.start()
        get_out.start()
        if last:
            keep_earlier = pltpu.make_async_copy(earlier, stash.at[0, micro - 1], sems.at[2])
            keep_earlier.start()
        @pl.loop(0, channels // LANES)
        def _(group):
            lanes = pl.ds(pl.multiple_of(group * LANES, LANES), LANES)
            inputs = [source(row, lanes) for row in range(rows + 2 * REACH)]
            for col in range(TAPS):
                parts = [None] * rows
                for off in range(TAPS):
                    tap = taps[off * TAPS + col, :, lanes]
                    tap = jnp.concatenate([tap] * (width // SUBLANES), axis=0)
                    for row in range(rows):
                        term = inputs[row + off] * tap
                        parts[row] = term if off == 0 else parts[row] + term
                for row in range(rows):
                    sums[row, col * width : (col + 1) * width, lanes] = parts[row]

        @pl.loop(0, rows, unroll=8)
        def _(row):
            conv = jnp.dot(select[...], sums[row], preferred_element_type=F32) + conv_bias[...]
            centred = conv - jnp.mean(conv, axis=-1, keepdims=True)
            var = jnp.mean(centred * centred, axis=-1, keepdims=True)
            normed = (centred * lax.rsqrt(var + 1e-06) * gain[...] + shift[...]).astype(BF)
            normal[pl.ds(pl.multiple_of(row * width, width), width), :] = normed

        get_in.wait()
        for start in range(0, hidden, chunk):
            part = slice(start, start + chunk)
            inner = jnp.dot(normal[...], w_in[:, part], preferred_element_type=F32) + inner_bias[:, part]
            act = (0.5 * inner * (1.0 + lax.erf(inner * np.float32(0.5**0.5)))).astype(BF)
            if start == 0:
                get_out.wait()
            branch = jnp.dot(act, w_out[part, :], preferred_element_type=F32)
            if start == 0:
                total[...] = branch
            else:
                total[...] += branch
        def outcome(row, value):
            branch = total[pl.ds(pl.multiple_of(row * width, width), width), :] + b_out[...]
            value = (value.astype(F32) + scale[...] * branch).astype(BF)
            result[own_row(flags[1], rows, row)] = value
            if last:
                keep(row).start()
            return value

        def keep(row):
            at = own_row(flags[1], rows, row)
            return pltpu.make_async_copy(result.at[at], stash.at[0, micro, at], sems.at[3])

        @pl.loop(0, NEAR, unroll=True)
        def _(row):
            value = outcome(row, near[row])
            if not final:
                near_out[row] = value

        @pl.loop(0, rows - NEAR, unroll=True)
        def _(row):
            value = outcome(row + NEAR, far[row])
            if not final:
                far_out[row] = value
                if rows - NEAR == CROSS:
                    cross_out[row] = value
                else:

                    @pl.when(row >= rows - NEAR - CROSS)
                    def _():
                        cross_out[jnp.maximum(row - (rows - NEAR - CROSS), 0)] = value

        if last:
            keep_earlier.wait()
            pltpu.make_async_copy(result, stash.at[0, micro], sems.at[3]).wait()


def run_block(micro, micros, final, flags, halo, params, weights, earlier, stash):
    last = micro == micros - 1
    near, far = halo[:2]
    rows, width, channels = near.shape[0] + far.shape[0], near.shape[1], near.shape[2]
    vmem = pl.BlockSpec(memory_space=pltpu.VMEM)
    anywhere = pl.BlockSpec(memory_space=pl.ANY)
    held = [pltpu.with_memory_space_constraint(v, pltpu.VMEM) for v in [*halo, *params]]
    pinned = [pltpu.with_memory_space_constraint(v, pltpu.HBM) for v in weights]
    operands = [flags] + held + pinned
    specs = [pl.BlockSpec(memory_space=pltpu.SMEM)] + [vmem] * len(held)
    specs += [pl.BlockSpec(memory_space=pltpu.HBM)] * len(pinned)
    counts = () if final else (NEAR, rows - NEAR, CROSS)
    out_shape = [pltpu.VMEM((count, width, channels), BF) for count in counts]
    scratch = [
        pltpu.VMEM(weights[0].shape, BF),
        pltpu.VMEM(weights[1].shape, BF),
        pltpu.VMEM((rows, TAPS * width, channels), BF),
        pltpu.VMEM((rows * width, channels), BF),
        pltpu.VMEM((rows * width, channels), F32),
    ]
    result = pltpu.VMEM((rows, width, channels), BF)
    out_specs = [vmem] * len(out_shape)
    aliases = {}
    if last:
        operands.append(pltpu.with_memory_space_constraint(earlier, pltpu.VMEM))
        specs.append(vmem)
        if stash is not None:
            aliases = {len(operands): len(out_shape)}
            operands.append(stash)
            specs.append(anywhere)
        out_shape.append(jax.ShapeDtypeStruct((1, micros, rows, width, channels), BF))
        out_specs.append(anywhere)
        scratch.append(result)
    else:
        out_shape.append(result)
        out_specs.append(vmem)
    *relayed, kept = pl.pallas_call(
        functools.partial(block_kernel, micro, last, final, 768),
        out_shape=out_shape,
        in_specs=specs,
        out_specs=out_specs,
        scratch_shapes=scratch + [pltpu.SemaphoreType.DMA((4,))],
        input_output_aliases=aliases,
        compiler_params=pltpu.CompilerParams(vmem_limit_bytes=32 * 2**20),
        cost_estimate=pl.CostEstimate(flops=2**20 if last else 2**33, bytes_accessed=2**10, transcendentals=0),
        name="block",
    )(*operands)
    return relayed, kept


def body(images, dw_weight, dw_bias, ln_gain, ln_bias, w_in, b_in, w_out, b_out, layer_scale):
    segment = lax.axis_index("segment")
    sections = lax.axis_size("segment")
    place = lax.axis_index("dp")
    places = lax.axis_size("dp")
    micros, rows, width, channels = images.shape
    per_image = SIDE // rows
    half = per_image // 2
    reverse = (place % 2 == 0).astype(jnp.int32)
    flags = [jnp.stack([(segment == section).astype(jnp.int32), reverse]) for section in range(sections)]

    axes = ("segment", "dp")

    def index(section, p):
        return section % sections * places + p % places

    facing = {}
    for p in range(places):
        if (p + half) % per_image in (half - 1, half):
            facing[p] = p + 1 if p % 2 == 1 else p - 1
    swap_pairs = [(index(s, p), index(s, p ^ 1)) for s in range(sections) for p in range(places)]
    near_pairs = [(index(s, p), index(s, q)) for s in range(sections) for p, q in facing.items()]

    def relay_pairs(section, onward):
        return [(index(section, p), index(section + 1, q)) for p, q in onward.items()]

    same = {p: p for p in range(places)}

    shape = (micros, CROSS, width, channels)
    cross = mirrored_rows(cross_kernel, "cross_rows", flags[0], images, [shape], micros * CROSS)[0]
    cross = lax.ppermute(cross, axes, near_pairs)
    shapes = [(NEAR, width, channels)] * micros + [(rows - NEAR, width, channels)] * micros
    parts = mirrored_rows(rows_kernel, "own_rows", flags[0], images, shapes, micros * rows)
    params = setup(flags[0], dw_weight, (dw_bias, ln_gain, ln_bias, b_out, layer_scale), b_in, width)
    weights = (w_in[0], w_out[0])

    halos = [(parts[m], parts[micros + m], cross) for m in range(micros)]
    stash = before = None
    for section in range(sections):
        later, earlier = [], None
        for m in range(micros):
            near, far, cross = halos[m]
            if section > 0:
                near, _ = lax.optimization_barrier((near, before))
            swap = lax.ppermute(near, axes, swap_pairs)
            halo = (near, far, swap, cross)
            final = section == sections - 1
            relayed, kept = run_block(m, micros, final, flags[section], halo, params, weights, earlier, stash)
            before = kept
            if m == micros - 1:
                stash = kept
            else:
                earlier = kept
            if not final:
                near = lax.ppermute(relayed[0], axes, relay_pairs(section, same))
                cross = lax.ppermute(relayed[2], axes, relay_pairs(section, facing))
                far = lax.ppermute(relayed[1], axes, relay_pairs(section, same))
                later.append((near, far, cross))
        halos = later
    return stash


def solution(mesh):
    in_specs = (
        P(None, "dp", None, None),
        P("segment", None, None, None),
        P("segment", None),
        P("segment", None),
        P("segment", None),
        P("segment", None, None),
        P("segment", None),
        P("segment", None, None),
        P("segment", None),
        P("segment", None),
    )
    out_specs = P("segment", None, "dp", None, None)
    return jax.shard_map(body, mesh=mesh, in_specs=in_specs, out_specs=out_specs, check_vma=False)
```

```python
import functools

import jax
import jax.numpy as jnp
import numpy as np
from jax import lax
from jax.experimental import pallas as pl
from jax.experimental.pallas import tpu as pltpu
from jax.sharding import PartitionSpec as P

SIDE = 32
TAPS = 7
REACH = 3
CROSS = 3
NEAR = 3
LANES = 128
SUBLANES = 16
BF = jnp.bfloat16
F32 = jnp.float32
VECTORS = 5


def own_row(flip, rows, row):
    return flip * (rows - 1) + (1 - 2 * flip) * row


def run_copies(copies, sems):
    copies = [pltpu.make_async_copy(a, b, sems.at[i]) for i, (a, b) in enumerate(copies)]
    for copy in copies:
        copy.start()
    return copies


def cross_kernel(flags, images, cross, sems):
    micros, rows = images.shape[:2]
    copies = []
    for m in range(micros):
        for row in range(rows - CROSS, rows):
            copies.append((images.at[m, own_row(flags[1], rows, row)], cross.at[m, row - (rows - CROSS)]))
    for copy in run_copies(copies, sems):
        copy.wait()


def rows_kernel(flags, images, *rest):
    micros, rows = images.shape[:2]
    sems = rest[-1]
    copies = []
    for m in range(micros):
        near, far = rest[m], rest[micros + m]
        for row in range(rows):
            here = images.at[m, own_row(flags[1], rows, row)]
            copies.append((here, near.at[row] if row < NEAR else far.at[row - NEAR]))
    for copy in run_copies(copies, sems):
        copy.wait()


def mirrored_rows(kernel, name, flags, images, shapes, copies):
    return pl.pallas_call(
        kernel,
        out_shape=[pltpu.VMEM(shape, BF) for shape in shapes],
        in_specs=[pl.BlockSpec(memory_space=pltpu.SMEM), pl.BlockSpec(memory_space=pltpu.HBM)],
        out_specs=[pl.BlockSpec(memory_space=pltpu.VMEM)] * len(shapes),
        scratch_shapes=[pltpu.SemaphoreType.DMA((copies,))],
        compiler_params=pltpu.CompilerParams(vmem_limit_bytes=2**20),
        cost_estimate=pl.CostEstimate(flops=0, bytes_accessed=2**21, transcendentals=0),
        name=name,
    )(flags, pltpu.with_memory_space_constraint(images, pltpu.HBM))


def setup_kernel(flags, weight, conv_bias, gain, shift, b_out, scale, b_in, taps, vectors, inner, select, raw, sems):
    copies = [(v, vectors.at[i]) for i, v in enumerate((conv_bias, gain, shift, b_out, scale))]
    copies += [(b_in, inner)]
    copies += [(weight.at[0, jnp.where(flags[1] == 1, TAPS - 1 - i, i)], raw.at[i]) for i in range(TAPS)]
    copies = run_copies(copies, sems)
    width, depth = select.shape
    at = lax.broadcasted_iota(jnp.int32, (width, depth), 0)
    entry = lax.broadcasted_iota(jnp.int32, (width, depth), 1)
    hit = jnp.zeros((width, depth), jnp.bool_)
    for col in range(TAPS):
        hit = hit | ((entry - col * width == at + col - REACH) & (entry >= col * width) & (entry < (col + 1) * width))
    select[...] = hit.astype(F32).astype(BF)
    for copy in copies:
        copy.wait()
    for off in range(TAPS):
        rows = raw[off].astype(F32)
        for col in range(TAPS):
            one = jnp.broadcast_to(rows[col : col + 1, :], (SUBLANES, rows.shape[1]))
            taps[off * TAPS + col] = one.astype(BF)


def setup(flags, weight, vectors, b_in, width):
    channels = weight.shape[-1]
    operands = [pltpu.with_memory_space_constraint(v, pltpu.HBM) for v in (weight, *vectors, b_in)]
    return pl.pallas_call(
        setup_kernel,
        out_shape=[
            pltpu.VMEM((TAPS * TAPS, SUBLANES, channels), BF),
            pltpu.VMEM((VECTORS, 1, channels), F32),
            pltpu.VMEM(b_in.shape, F32),
            pltpu.VMEM((width, TAPS * width), BF),
        ],
        in_specs=[pl.BlockSpec(memory_space=pltpu.SMEM)] + [pl.BlockSpec(memory_space=pltpu.HBM)] * len(operands),
        out_specs=[pl.BlockSpec(memory_space=pltpu.VMEM)] * 4,
        scratch_shapes=[
            pltpu.VMEM((TAPS, TAPS, channels), BF),
            pltpu.SemaphoreType.DMA((VECTORS + 1 + TAPS,)),
        ],
        compiler_params=pltpu.CompilerParams(vmem_limit_bytes=4 * 2**20),
        cost_estimate=pl.CostEstimate(flops=0, bytes_accessed=2**22, transcendentals=0),
        name="setup",
    )(flags, *operands)


def block_kernel(micro, last, final, chunk, *refs):
    refs = list(refs)
    flags, near, far, swap, cross, taps, vectors, inner_bias, select, w_in_hbm, w_out_hbm = refs[:11]
    w_in, w_out, sums, normal, total, *tail = refs[-7 if last else -6 :]
    sems = tail[-1]
    outs = refs[11 : -7 if last else -6]
    if last:
        earlier, stash, result = outs[0], outs[-1], tail[0]
    else:
        result = outs[-1]
    near_out, far_out, cross_out = (None, None, None) if final else outs[-4:-1]
    rows, width, channels = near.shape[0] + far.shape[0], near.shape[1], near.shape[2]
    cross = cross.at[micro] if len(cross.shape) == 4 else cross
    hidden = w_in.shape[1]
    conv_bias, gain, shift, b_out, scale = (vectors.at[i] for i in range(VECTORS))

    def source(row, lanes):
        if row < REACH:
            return swap[REACH - 1 - row, :, lanes]
        if row < REACH + NEAR:
            return near[row - REACH, :, lanes]
        if row < REACH + rows:
            return far[row - REACH - NEAR, :, lanes]
        return cross[REACH + CROSS + rows - 1 - row, :, lanes]

    @pl.when(flags[0] == 1)
    def _():
        get_in = pltpu.make_async_copy(w_in_hbm, w_in, sems.at[0])
        get_out = pltpu.make_async_copy(w_out_hbm, w_out, sems.at[1])
        get_in.start()
        get_out.start()
        if last:
            keep_earlier = pltpu.make_async_copy(earlier, stash.at[0, micro - 1], sems.at[2])
        @pl.loop(0, channels // LANES)
        def _(group):
            lanes = pl.ds(pl.multiple_of(group * LANES, LANES), LANES)
            inputs = [source(row, lanes) for row in range(rows + 2 * REACH)]
            for col in range(TAPS):
                parts = [None] * rows
                for off in range(TAPS):
                    tap = taps[off * TAPS + col, :, lanes]
                    tap = jnp.concatenate([tap] * (width // SUBLANES), axis=0)
                    for row in range(rows):
                        term = inputs[row + off] * tap
                        parts[row] = term if off == 0 else parts[row] + term
                for row in range(rows):
                    sums[row, col * width : (col + 1) * width, lanes] = parts[row]

        @pl.loop(0, rows, unroll=8)
        def _(row):
            conv = jnp.dot(select[...], sums[row], preferred_element_type=F32) + conv_bias[...]
            centred = conv - jnp.mean(conv, axis=-1, keepdims=True)
            var = jnp.mean(centred * centred, axis=-1, keepdims=True)
            normed = (centred * lax.rsqrt(var + 1e-06) * gain[...] + shift[...]).astype(BF)
            normal[pl.ds(pl.multiple_of(row * width, width), width), :] = normed

        get_in.wait()
        if last:
            keep_earlier.start()
        for start in range(0, hidden, chunk):
            part = slice(start, start + chunk)
            inner = jnp.dot(normal[...], w_in[:, part], preferred_element_type=F32) + inner_bias[:, part]
            act = (0.5 * inner * (1.0 + lax.erf(inner * np.float32(0.5**0.5)))).astype(BF)
            if start == 0:
                get_out.wait()
            branch = jnp.dot(act, w_out[part, :], preferred_element_type=F32)
            if start == 0:
                total[...] = branch
            else:
                total[...] += branch
        def outcome(row, value):
            branch = total[pl.ds(pl.multiple_of(row * width, width), width), :] + b_out[...]
            value = (value.astype(F32) + scale[...] * branch).astype(BF)
            result[own_row(flags[1], rows, row)] = value
            if last:
                keep(row).start()
            return value

        def keep(row):
            at = own_row(flags[1], rows, row)
            return pltpu.make_async_copy(result.at[at], stash.at[0, micro, at], sems.at[3])

        @pl.loop(0, NEAR, unroll=True)
        def _(row):
            value = outcome(row, near[row])
            if not final:
                near_out[row] = value

        @pl.loop(0, rows - NEAR, unroll=True)
        def _(row):
            value = outcome(row + NEAR, far[row])
            if not final:
                far_out[row] = value
                if rows - NEAR == CROSS:
                    cross_out[row] = value
                else:

                    @pl.when(row >= rows - NEAR - CROSS)
                    def _():
                        cross_out[jnp.maximum(row - (rows - NEAR - CROSS), 0)] = value

        if last:
            keep_earlier.wait()
            pltpu.make_async_copy(result, stash.at[0, micro], sems.at[3]).wait()


def run_block(micro, micros, final, flags, halo, params, weights, earlier, stash):
    last = micro == micros - 1
    near, far = halo[:2]
    rows, width, channels = near.shape[0] + far.shape[0], near.shape[1], near.shape[2]
    vmem = pl.BlockSpec(memory_space=pltpu.VMEM)
    anywhere = pl.BlockSpec(memory_space=pl.ANY)
    held = [pltpu.with_memory_space_constraint(v, pltpu.VMEM) for v in [*halo, *params]]
    pinned = [pltpu.with_memory_space_constraint(v, pltpu.HBM) for v in weights]
    operands = [flags] + held + pinned
    specs = [pl.BlockSpec(memory_space=pltpu.SMEM)] + [vmem] * len(held)
    specs += [pl.BlockSpec(memory_space=pltpu.HBM)] * len(pinned)
    counts = () if final else (NEAR, rows - NEAR, CROSS)
    out_shape = [pltpu.VMEM((count, width, channels), BF) for count in counts]
    scratch = [
        pltpu.VMEM(weights[0].shape, BF),
        pltpu.VMEM(weights[1].shape, BF),
        pltpu.VMEM((rows, TAPS * width, channels), BF),
        pltpu.VMEM((rows * width, channels), BF),
        pltpu.VMEM((rows * width, channels), F32),
    ]
    result = pltpu.VMEM((rows, width, channels), BF)
    out_specs = [vmem] * len(out_shape)
    aliases = {}
    if last:
        operands.append(pltpu.with_memory_space_constraint(earlier, pltpu.VMEM))
        specs.append(vmem)
        if stash is not None:
            aliases = {len(operands): len(out_shape)}
            operands.append(stash)
            specs.append(anywhere)
        out_shape.append(jax.ShapeDtypeStruct((1, micros, rows, width, channels), BF))
        out_specs.append(anywhere)
        scratch.append(result)
    else:
        out_shape.append(result)
        out_specs.append(vmem)
    *relayed, kept = pl.pallas_call(
        functools.partial(block_kernel, micro, last, final, 768),
        out_shape=out_shape,
        in_specs=specs,
        out_specs=out_specs,
        scratch_shapes=scratch + [pltpu.SemaphoreType.DMA((4,))],
        input_output_aliases=aliases,
        compiler_params=pltpu.CompilerParams(vmem_limit_bytes=32 * 2**20),
        cost_estimate=pl.CostEstimate(flops=2**20 if last else 2**33, bytes_accessed=2**10, transcendentals=0),
        name="block",
    )(*operands)
    return relayed, kept


def body(images, dw_weight, dw_bias, ln_gain, ln_bias, w_in, b_in, w_out, b_out, layer_scale):
    segment = lax.axis_index("segment")
    sections = lax.axis_size("segment")
    place = lax.axis_index("dp")
    places = lax.axis_size("dp")
    micros, rows, width, channels = images.shape
    per_image = SIDE // rows
    half = per_image // 2
    reverse = (place % 2 == 0).astype(jnp.int32)
    flags = [jnp.stack([(segment == section).astype(jnp.int32), reverse]) for section in range(sections)]

    axes = ("segment", "dp")

    def index(section, p):
        return section % sections * places + p % places

    facing = {}
    for p in range(places):
        if (p + half) % per_image in (half - 1, half):
            facing[p] = p + 1 if p % 2 == 1 else p - 1
    swap_pairs = [(index(s, p), index(s, p ^ 1)) for s in range(sections) for p in range(places)]
    near_pairs = [(index(s, p), index(s, q)) for s in range(sections) for p, q in facing.items()]

    def relay_pairs(section, onward):
        return [(index(section, p), index(section + 1, q)) for p, q in onward.items()]

    same = {p: p for p in range(places)}

    shape = (micros, CROSS, width, channels)
    cross = mirrored_rows(cross_kernel, "cross_rows", flags[0], images, [shape], micros * CROSS)[0]
    cross = lax.ppermute(cross, axes, near_pairs)
    shapes = [(NEAR, width, channels)] * micros + [(rows - NEAR, width, channels)] * micros
    parts = mirrored_rows(rows_kernel, "own_rows", flags[0], images, shapes, micros * rows)
    params = setup(flags[0], dw_weight, (dw_bias, ln_gain, ln_bias, b_out, layer_scale), b_in, width)
    weights = (w_in[0], w_out[0])

    halos = [(parts[m], parts[micros + m], cross) for m in range(micros)]
    stash = before = None
    for section in range(sections):
        later, earlier = [], None
        for m in range(micros):
            near, far, cross = halos[m]
            if section > 0:
                near, _ = lax.optimization_barrier((near, before))
            swap = lax.ppermute(near, axes, swap_pairs)
            halo = (near, far, swap, cross)
            final = section == sections - 1
            relayed, kept = run_block(m, micros, final, flags[section], halo, params, weights, earlier, stash)
            before = kept
            if m == micros - 1:
                stash = kept
            else:
                earlier = kept
            if not final:
                near = lax.ppermute(relayed[0], axes, relay_pairs(section, same))
                cross = lax.ppermute(relayed[2], axes, relay_pairs(section, facing))
                far = lax.ppermute(relayed[1], axes, relay_pairs(section, same))
                later.append((near, far, cross))
        halos = later
    return stash


def solution(mesh):
    in_specs = (
        P(None, "dp", None, None),
        P("segment", None, None, None),
        P("segment", None),
        P("segment", None),
        P("segment", None),
        P("segment", None, None),
        P("segment", None),
        P("segment", None, None),
        P("segment", None),
        P("segment", None),
    )
    out_specs = P("segment", None, "dp", None, None)
    return jax.shard_map(body, mesh=mesh, in_specs=in_specs, out_specs=out_specs, check_vma=False)
```
